32 devices in a mesh: expert: 8 (over y, x, core), dp: 4 (over z).
Axes of the slice: x: 2, y: 2, z: 4, core: 2. Of those that a mesh axis runs over, the one named last changes fastest.
Arguments:
- tokens: bfloat16 [512, 2048], P(('expert', 'dp')), may hold values from -6 to 6
- cotangent: bfloat16 [512, 2048], P(('expert', 'dp')), may hold values from -6 to 6
- route_ids: int32 [512, 8], P(('expert', 'dp')), may hold values from 0 to 7, all different within a row; in each aligned block of 16 rows (0 to 15, 16 to 31, ...) at most 16 rows name the same one
- route_gates: bfloat16 [512, 8], P(('expert', 'dp')), may hold values from 0.019897461 to 0.5
- gate_up: bfloat16 [8, 2048, 1536], P('expert', 'dp'), may hold values from -0.125 to 0.125
- down: bfloat16 [8, 2048, 768], P('expert', 'dp'), may hold values from -6 to 6
- moment1: bfloat16 [8, 2048, 768], P('expert', 'dp'), may hold values from -4 to 4
- moment2: bfloat16 [8, 2048, 768], P('expert', 'dp'), may hold values from 0.049804688 to 0.5
- placement: int32 [8], replicated, may hold values from 0 to 7, each once
Outputs:
- rollout_down: bfloat16 [8, 2048, 768], P('expert', None, 'dp')
The draws below stay inside these ranges and needn't reach their ends.
Inputs may be any that keep to these rules, and one draw needn't show every extreme that they name: `route_ids`: each row names 8 different experts; within the rows of one device no expert is named more than 16 times, a bound that some block reaches. `placement`: each expert exactly once.
All inputs are finite; a program needn't handle non-finite values.
Results may differ from the reference program's by a relative error of at most 0.003.
Values may be sent and summed in bfloat16 or wider, within the bound.
No kernel may reach another device: no remote copies, remote signals or barrier semaphores. Data moves between devices by JAX's collectives and lax.ppermute only.
A program may use at most 64 MiB of HBM per device.

```python
import math
import jax
import jax.numpy as jnp
import numpy as np
from jax import lax

D = 2048
H = 768
TOP = 8
OPT_STEP = 2
TOK_DEV = 16
EXPERTS = 8
CAP = 16
TOKENS = 512
N_EXPERT = 8
N_DP = 4


def shard_levels(stream_key, extent, pieces, least, high):
    def one(dim, parts):
        heights = jax.random.uniform(jax.random.fold_in(jax.random.fold_in(stream_key, 6), dim), (parts,), jnp.float32, least / len(pieces), high / len(pieces))
        return jnp.repeat(jnp.exp(heights), extent[dim] // parts).reshape((-1,) + (1,) * (len(extent) - dim - 1))

    loudness = one(*pieces[0])
    for cut in pieces[1:]:
        loudness = loudness * one(*cut)
    return loudness


def routed_block(stream_key, own, number, rows, amount, top, bound, lean):
    sequence = jax.random.permutation(stream_key, amount)
    packed, common = portions_of(amount, rows * top, bound, lean, True), portions_of(amount, rows * top, bound, lean, False)
    places = jnp.arange(amount)

    def named(tallies, offset_by):
        used = int((tallies > 0).sum())
        fixed = max(1, used // 4)
        shifted = fixed + (places - fixed + offset_by * (used - fixed)) % max(1, amount - fixed)
        return jnp.zeros((amount,), jnp.int32).at[sequence[jnp.where(places < fixed, places, shifted)]].set(jnp.asarray(tallies, jnp.int32))

    tallies = jnp.where(number % 4 == 0, named(packed, number // 4), named(common, number - number // 4 - 1))
    mixed = jax.random.permutation(jax.random.fold_in(own, 3), amount)
    source_of, taker = mixed[0:amount // 2 * 2:2], mixed[1:amount // 2 * 2:2]
    slack = jnp.minimum(tallies[source_of] - 1, bound - tallies[taker]) // 2
    slack = jnp.where((source_of == sequence[0]) | (taker == sequence[0]) | (tallies[taker] == 0), 0, jnp.maximum(slack, 0))
    shifted = jax.random.randint(jax.random.fold_in(own, 4), (amount // 2,), 0, 1 << 20) % (slack + 1)
    tallies = tallies.at[source_of].add(-shifted).at[taker].add(shifted)
    labels = jnp.searchsorted(jnp.cumsum(tallies), jnp.arange(rows * top), side="right").astype(jnp.int32)
    listing = labels.reshape(top, rows).T
    listing = listing[jax.random.permutation(jax.random.fold_in(own, 1), rows)]
    offset_by = jax.random.randint(jax.random.fold_in(own, 2), (rows, 1), 0, top)
    return jnp.take_along_axis(listing, (jnp.arange(top)[None, :] + offset_by) % top, axis=1)


def portions_of(count, total, most, skew, full):
    loads = [(1 << 20) // math.isqrt(standing ** skew) + 1 for standing in range(1, count + 1)]
    largest = most if full else min(most, max(-(-total // count), total * loads[0] // sum(loads)))
    least = 1 if total - largest >= count - 1 else 0
    given, spare = [largest] + [least] * (count - 1), total - largest - least * (count - 1)
    while spare > 0:
        free = [i for i in range(1, count) if given[i] < largest] or [i for i in range(1, count) if given[i] < most]
        pool, remaining = sum([loads[i] for i in free]), spare
        for i in free:
            extra = min(most - given[i], max(1, remaining * loads[i] // pool), spare)
            given[i] = given[i] + extra
            spare = spare - extra
    return np.array(given)


def gaussian(stream_key, extent, spread, reach, cuts=(), kind=jnp.bfloat16):
    result = jax.random.normal(stream_key, extent, jnp.float32) * spread
    if len(cuts) > 0:
        result = shard_levels(stream_key, extent, cuts, -0.22, 0.18) * result
    return jnp.clip(result, min=-reach, max=reach).astype(kind)


def setup_inputs(seed: int = 0) -> dict:
    seeds = jax.random.split(jax.random.key(seed), 10)
    tokens = gaussian(seeds[0], (TOKENS, D), 1.0, 6.0, ((0, 32),))
    cotangent = gaussian(seeds[1], (TOKENS, D), 1.0, 6.0, ((0, 32),))
    route_ids_keys = jax.random.split(jax.random.fold_in(seeds[2], 1), TOKENS // TOK_DEV)
    route_ids_turns = jax.random.permutation(jax.random.fold_in(seeds[2], 3), TOKENS // TOK_DEV)
    route_ids = jax.vmap(lambda own, number: routed_block(jax.random.fold_in(seeds[2], 2), own, number, TOK_DEV, EXPERTS, TOP, CAP, 2))(route_ids_keys, route_ids_turns).reshape((TOKENS, TOP))
    route_gates = jnp.clip(jnp.exp(math.log(0.5) - 3.224016 * jax.random.uniform(seeds[3], (TOKENS, TOP), jnp.float32) ** shard_levels(seeds[3], (TOKENS, TOP), ((0, 32),), -0.2, 0.2)), 0.019897461, 0.5).astype(jnp.bfloat16)
    gate_up = gaussian(seeds[4], (EXPERTS, D, 2 * H), D ** -0.5, 0.125, ((0, 8), (1, 4)))
    down = gaussian(seeds[5], (EXPERTS, D, H), 1.0, 6.0, ((0, 8), (1, 4)))
    moment1 = gaussian(seeds[6], (EXPERTS, D, H), 0.3, 4.0, ((0, 8), (1, 4)))
    moment2 = jnp.clip(jnp.exp(math.log(0.5) - 2.306499 * jax.random.uniform(seeds[7], (EXPERTS, D, H), jnp.float32) ** shard_levels(seeds[7], (EXPERTS, D, H), ((0, 8), (1, 4)), -0.2, 0.2)), 0.049804688, 0.5).astype(jnp.bfloat16)
    placement = jax.random.permutation(seeds[8], EXPERTS).astype(jnp.int32)
    return {"tokens": tokens, "cotangent": cotangent, "route_ids": route_ids, "route_gates": route_gates, "gate_up": gate_up, "down": down, "moment1": moment1, "moment2": moment2, "placement": placement}


BETA_ONE = 0.9
BETA_TWO = 0.95
ADAM_EPS = 1e-08
LEARN_RATE = 0.25

def reference(tokens, cotangent, route_ids, route_gates, gate_up, down, moment1, moment2, placement):
    blocks = N_EXPERT * N_DP
    route_table = route_ids.reshape(blocks, TOK_DEV, TOP)
    route_hits = lax.optimization_barrier(jnp.sum((route_table[:, :, :, None] == jnp.arange(EXPERTS, dtype=jnp.int32)).astype(jnp.int32), axis=2))
    earlier_hits = jnp.cumsum(route_hits, axis=1) - route_hits
    slot_index = jnp.take_along_axis(earlier_hits, route_table, axis=2).astype(jnp.int32)
    row_ids = jnp.broadcast_to(jnp.arange(TOKENS, dtype=jnp.int32).reshape(blocks, TOK_DEV, 1), route_table.shape)
    owner_block = jnp.broadcast_to(jnp.arange(blocks, dtype=jnp.int32).reshape(blocks, 1, 1), route_table.shape)
    slot_rows = jnp.full((EXPERTS, blocks, CAP), TOKENS, jnp.int32).at[route_table, owner_block, slot_index].set(row_ids)
    slot_gates = jnp.zeros((EXPERTS, blocks, CAP), jnp.float32).at[route_table, owner_block, slot_index].set(route_gates.reshape(blocks, TOK_DEV, TOP).astype(jnp.float32))
    slot_rows = slot_rows.reshape(EXPERTS, N_EXPERT, N_DP, CAP).transpose(0, 2, 1, 3).reshape(EXPERTS, N_DP, N_EXPERT * CAP)
    slot_gates = slot_gates.reshape(EXPERTS, N_EXPERT, N_DP, CAP).transpose(0, 2, 1, 3).reshape(EXPERTS, N_DP, N_EXPERT * CAP)
    padded_rows = jnp.concatenate([tokens, jnp.zeros((1, D), tokens.dtype)], axis=0)
    padded_grads = jnp.concatenate([cotangent, jnp.zeros((1, D), cotangent.dtype)], axis=0)
    correct_one = 1.0 - BETA_ONE ** OPT_STEP
    correct_two = 1.0 - BETA_TWO ** OPT_STEP

    def per_expert(inputs):
        rows_e, gates_e, weights_e, down_e, first_e, second_e = inputs

        def per_group(running, group_data):
            rows_g, gates_g = group_data
            gathered = padded_rows[rows_g]
            pre = jnp.dot(gathered, weights_e, preferred_element_type=jnp.float32)
            hidden = (jax.nn.silu(pre[:, :H]) * pre[:, H:]).astype(jnp.bfloat16)
            scaled = (gates_g[:, None] * padded_grads[rows_g].astype(jnp.float32)).astype(jnp.bfloat16)
            partial_value = jnp.dot(scaled.T, hidden, preferred_element_type=jnp.float32)
            partial_value = lax.optimization_barrier(partial_value.astype(jnp.bfloat16)).astype(jnp.float32)
            return (running + partial_value, None)
        grad_sum, _ = lax.scan(per_group, jnp.zeros((D, H), jnp.float32), (rows_e, gates_e))
        first = BETA_ONE * first_e.astype(jnp.float32) + (1.0 - BETA_ONE) * grad_sum
        second = BETA_TWO * second_e.astype(jnp.float32) + (1.0 - BETA_TWO) * grad_sum * grad_sum
        direction = first / correct_one / (jnp.sqrt(second / correct_two) + ADAM_EPS)
        updated = down_e.astype(jnp.float32) - LEARN_RATE * direction
        return updated.astype(jnp.bfloat16)
    updated_all = lax.map(per_expert, (slot_rows, slot_gates, gate_up, down, moment1, moment2))
    return jnp.take(updated_all, placement, axis=0)
```

```python
import functools

import jax
import jax.numpy as jnp
from jax import lax
from jax.experimental import pallas as pl
from jax.experimental.pallas import tpu as pltpu
from jax.sharding import PartitionSpec as P

OPT_STEP = 2


BETA_ONE = 0.9
BETA_TWO = 0.95
ADAM_EPS = 1e-08
LEARN_RATE = 0.25

BF16 = jnp.bfloat16
F32 = jnp.float32
LANES = 128
HALF = LANES // 2


def adam(down, moment1, moment2, grad):
    correct_one = 1.0 - BETA_ONE**OPT_STEP
    correct_two = 1.0 - BETA_TWO**OPT_STEP
    first = BETA_ONE * moment1.astype(F32) + (1.0 - BETA_ONE) * grad
    second = BETA_TWO * moment2.astype(F32) + (1.0 - BETA_TWO) * grad * grad
    direction = first / correct_one / (jnp.sqrt(second / correct_two) + ADAM_EPS)
    return (down.astype(F32) - LEARN_RATE * direction).astype(BF16)


def routed(tokens, cotangent, route_ids, route_gates, gate_up, down, moment1, moment2, placement):
    experts = lax.axis_size("expert")
    tok_rows = tokens.shape[0]
    width = tokens.shape[1]
    top_count = route_ids.shape[1]
    hidden_units = down.shape[2]
    capacity = min(tok_rows, 2 * tok_rows * top_count // experts)
    total_slots = experts * capacity
    route_hits = jnp.sum(
        (route_ids[:, :, None] == jnp.arange(experts, dtype=jnp.int32)).astype(jnp.int32), axis=1
    )
    earlier_hits = jnp.cumsum(route_hits, axis=0) - route_hits
    slot_index = jnp.take_along_axis(earlier_hits, route_ids, axis=1)
    target_slot = route_ids * capacity + slot_index
    matched = (target_slot[:, :, None] == jnp.arange(total_slots, dtype=jnp.int32)).astype(F32)
    picker = jnp.sum(matched, axis=1).astype(BF16)
    contract_rows = (((0,), (0,)), ((), ()))
    send_rows = lax.dot_general(picker, tokens, contract_rows, preferred_element_type=F32)
    send_rows = send_rows.astype(BF16).reshape(experts, capacity, width)
    send_grads = lax.dot_general(picker, cotangent, contract_rows, preferred_element_type=F32)
    send_grads = send_grads.astype(BF16).reshape(experts, capacity, width)
    send_gates = jnp.sum(matched * route_gates.astype(F32)[:, :, None], axis=(0, 1))
    send_gates = send_gates.astype(BF16).reshape(experts, capacity)
    rows_in, grads_in, gates_in = (
        lax.all_to_all(send_rows, "expert", split_axis=0, concat_axis=0, tiled=True),
        lax.all_to_all(send_grads, "expert", split_axis=0, concat_axis=0, tiled=True),
        lax.all_to_all(send_gates, "expert", split_axis=0, concat_axis=0, tiled=True),
    )
    pre_all = jnp.dot(
        rows_in.reshape(total_slots, width),
        lax.all_gather(gate_up, "dp", axis=1, tiled=True)[0],
        preferred_element_type=F32,
    )
    hidden = (jax.nn.silu(pre_all[:, :hidden_units]) * pre_all[:, hidden_units:]).astype(BF16)
    scaled = gates_in.reshape(total_slots, 1).astype(F32) * grads_in.reshape(
        total_slots, width
    ).astype(F32)
    partial = lax.dot_general(
        scaled.astype(BF16), hidden, contract_rows, preferred_element_type=F32
    ).astype(BF16)
    grad_share = lax.psum_scatter(partial, "dp", scatter_dimension=0, tiled=True).astype(F32)
    updated = adam(down[0], moment1[0], moment2[0], grad_share)
    column_block = lax.all_to_all(updated, "dp", split_axis=1, concat_axis=0, tiled=True)
    block_cols = column_block.shape[1]
    piece_flat = column_block.reshape(experts, width * block_cols // experts)
    spread = lax.all_to_all(piece_flat, "expert", split_axis=0, concat_axis=0, tiled=True)
    picked = jnp.take(spread, placement, axis=0)
    landed = lax.all_to_all(picked, "expert", split_axis=0, concat_axis=0, tiled=True)
    return landed.reshape(1, width, block_cols)


def partner(x, axis, flip):
    size = lax.axis_size(axis)
    return lax.ppermute(x, axis, [(i, i ^ flip) for i in range(size)])


def vmem(*shape_and_index):
    return pl.BlockSpec(*shape_and_index)


def smem():
    return pl.BlockSpec(memory_space=pltpu.SMEM)


def pack_rows_kernel(place, tok, cot, ids, gates, *outs):
    groups = len(outs)
    width = tok.shape[1]
    block = width // groups
    group = place[1]
    lane = lax.broadcasted_iota(jnp.int32, (tok.shape[0], LANES), 1)
    dense = jnp.zeros(lane.shape, F32)
    named = ids[...]
    weights = gates[...].astype(F32)
    for k in range(named.shape[1]):
        dense = dense + jnp.where(lane == named[:, k : k + 1], weights[:, k : k + 1], 0.0)
    dense = dense.astype(BF16)
    for flip, out in enumerate(outs):
        start = pl.multiple_of((group ^ flip) * block, LANES)
        out[:, :width] = tok[...]
        out[:, width : width + block] = cot[:, pl.ds(start, block)]
        out[:, width + block :] = dense


def pack_rows(place, tokens, cotangent, ids, gates, groups):
    rows, width = tokens.shape
    shape = jax.ShapeDtypeStruct((rows, width + width // groups + LANES), BF16)
    return pl.pallas_call(
        pack_rows_kernel,
        out_shape=[shape] * groups,
        in_specs=[smem()] + [pl.BlockSpec(memory_space=pltpu.VMEM)] * 4,
        name="pack_rows",
    )(place, tokens, cotangent, ids, gates)


def swap_halves(x):
    return jnp.concatenate([x[:, HALF:], x[:, :HALF]], axis=1)


def pack_weights_kernel(place, weights, *outs):
    groups = len(outs)
    hidden_units = weights.shape[1] // 2
    group = place[1]
    for flip, out in enumerate(outs):
        col = group ^ flip
        whole = pl.multiple_of(col * LANES, LANES)
        out[:, :LANES] = weights[:, pl.ds(whole, LANES)]
        out[:, LANES : 2 * LANES] = weights[
            :, pl.ds(pl.multiple_of(hidden_units + whole, LANES), LANES)
        ]
        shared = pl.multiple_of(groups * LANES + (col // 2) * LANES, LANES)
        gate = weights[:, pl.ds(shared, LANES)]
        up = weights[:, pl.ds(pl.multiple_of(hidden_units + shared, LANES), LANES)]

        @pl.when(col % 2 == 0)
        def _():
            out[:, 2 * LANES :] = jnp.concatenate([gate[:, :HALF], up[:, :HALF]], axis=1)

        @pl.when(col % 2 == 1)
        def _():
            out[:, 2 * LANES :] = jnp.concatenate([gate[:, HALF:], up[:, HALF:]], axis=1)


def pack_weights(place, weights, groups):
    rows, cols = weights.shape
    shape = jax.ShapeDtypeStruct((rows, cols // groups), BF16)
    return pl.pallas_call(
        pack_weights_kernel,
        out_shape=[shape] * groups,
        in_specs=[smem(), pl.BlockSpec(memory_space=pltpu.VMEM)],
        name="pack_weights",
    )(place, weights)


def order_groups_kernel(place, *refs):
    *blocks, out = refs
    for flip, block in enumerate(blocks):
        out[pl.ds(place[1] ^ flip, 1)] = block[...][None]


def order_groups(place, blocks):
    rows, width = blocks[0].shape
    out = pl.pallas_call(
        order_groups_kernel,
        out_shape=jax.ShapeDtypeStruct((len(blocks), rows, width), BF16),
        in_specs=[smem()] + [pl.BlockSpec(memory_space=pltpu.VMEM)] * len(blocks),
        name="order_groups",
    )(place, *blocks)
    return out.reshape(len(blocks) * rows, width)


def hidden_kernel(groups, pieces, place, *refs):
    row_refs, weight_refs, out, toks = refs[:pieces], refs[pieces:-2], refs[-2], refs[-1]
    rows, width = row_refs[0].shape
    block = width // groups
    total = pieces * rows
    for i, ref in enumerate(row_refs):
        toks[i * rows : (i + 1) * rows, :] = ref[...]
    pre = None
    for flip, ref in enumerate(weight_refs):
        start = pl.multiple_of((place[1] ^ flip) * block, LANES)
        term = jnp.dot(toks[:, pl.ds(start, block)], ref[...], preferred_element_type=F32)
        pre = term if pre is None else pre + term
    gate, up = pre[:, :LANES], pre[:, LANES : 2 * LANES]
    out[:total, :] = (gate / (1.0 + jnp.exp(-gate)) * up).astype(BF16)
    gate, up = pre[:, 2 * LANES : 2 * LANES + HALF], pre[:, 2 * LANES + HALF :]
    narrow = (gate / (1.0 + jnp.exp(-gate)) * up).astype(BF16)
    out[total:, :] = jnp.concatenate([narrow[: total // 2], narrow[total // 2 :]], axis=1)


def hidden_blocks(place, pieces, weights, width):
    groups = len(weights)
    rows = pieces[0].shape[0]
    total = rows * len(pieces)
    return pl.pallas_call(
        functools.partial(hidden_kernel, groups, len(pieces)),
        out_shape=jax.ShapeDtypeStruct((total + total // 2, LANES), BF16),
        grid=(1,),
        in_specs=[smem()]
        + [pl.BlockSpec((rows, width), lambda i: (0, 0))] * len(pieces)
        + [pl.BlockSpec(weights[0].shape, lambda i: (0, 0))] * groups,
        out_specs=pl.BlockSpec((total + total // 2, LANES), lambda i: (0, 0)),
        scratch_shapes=[pltpu.VMEM((total, width), BF16)],
        compiler_params=pltpu.CompilerParams(vmem_limit_bytes=48 * 1024 * 1024),
        name="hidden_blocks",
    )(place, *pieces, *weights)


def scaled_kernel(pieces, place, *refs):
    cot_refs, gate_refs, out = refs[:pieces], refs[pieces:-1], refs[-1]
    rows = cot_refs[0].shape[0]
    for i in range(pieces):
        gates = gate_refs[i][...].astype(F32)
        lane = lax.broadcasted_iota(jnp.int32, gates.shape, 1)
        gate = jnp.sum(jnp.where(lane == place[0], gates, 0.0), axis=1, keepdims=True)
        out[i * rows : (i + 1) * rows, :] = (gate * cot_refs[i][...].astype(F32)).astype(BF16)


def scaled_rows(place, pieces, width, block):
    rows = pieces[0].shape[0]
    return pl.pallas_call(
        functools.partial(scaled_kernel, len(pieces)),
        out_shape=jax.ShapeDtypeStruct((rows * len(pieces), block), BF16),
        grid=(1,),
        in_specs=[smem()]
        + [pl.BlockSpec((rows, block), lambda i: (0, width // block))] * len(pieces)
        + [pl.BlockSpec((rows, LANES), lambda i: (0, (width + block) // LANES))] * len(pieces),
        out_specs=pl.BlockSpec((rows * len(pieces), block), lambda i: (0, 0)),
        name="scaled_rows",
    )(place, *pieces, *pieces)


def update_kernel(groups, places, place, *refs):
    hid_refs, (scaled, down, first, second, out, hidden) = refs[:groups], refs[groups:]
    total = scaled.shape[0]
    features, units = down.shape
    cols = units // groups

    @pl.when(pl.program_id(0) == 0)
    def _():
        for own in range(groups):

            @pl.when(place[1] == own)
            def _():
                for col in range(groups):
                    ref = hid_refs[own ^ col]
                    hidden[:, col * LANES : (col + 1) * LANES] = ref[:total, :]
                    start = groups * LANES + col * HALF
                    hidden[: total // 2, start : start + HALF] = ref[total:, :HALF]
                    hidden[total // 2 :, start : start + HALF] = ref[total:, HALF:]

    grad = lax.dot_general(
        scaled[...], hidden[...], (((0,), (0,)), ((), ())), preferred_element_type=F32
    )
    updated = adam(down[...], first[...], second[...], grad)
    step = features // places
    for i in range(places):
        rows = updated[i * step : (i + 1) * step]
        for col in range(groups):
            piece = rows[:, col * cols : (col + 1) * cols]
            narrow = piece[:, LANES:]
            out[i * groups + col, :step, :] = piece[:, :LANES]
            out[i * groups + col, step:, :] = jnp.concatenate(
                [narrow[: step // 2], narrow[step // 2 :]], axis=1
            )


def update_pieces(place, hidden, scaled, down, first, second, experts):
    groups = len(hidden)
    total, features = scaled.shape
    units = down.shape[1]
    steps = 4
    chunk = features // steps
    places = experts // steps
    piece_rows = features // experts * (units // groups) // LANES
    return pl.pallas_call(
        functools.partial(update_kernel, groups, places),
        out_shape=jax.ShapeDtypeStruct((experts * groups, piece_rows, LANES), BF16),
        grid=(steps,),
        in_specs=[smem()]
        + [pl.BlockSpec(hidden[0].shape, lambda i: (0, 0))] * groups
        + [pl.BlockSpec((total, chunk), lambda i: (0, i))]
        + [pl.BlockSpec((chunk, units), lambda i: (i, 0))] * 3,
        out_specs=pl.BlockSpec((places * groups, piece_rows, LANES), lambda i: (i, 0, 0)),
        scratch_shapes=[pltpu.VMEM((total, units), BF16)],
        compiler_params=pltpu.CompilerParams(vmem_limit_bytes=48 * 1024 * 1024),
        name="update_pieces",
    )(place, *hidden, scaled, down, first, second)


def copy_kernel(order, x, out):
    out[...] = x[...]


def reorder(order, x):
    block = (1,) + x.shape[1:]
    return pl.pallas_call(
        copy_kernel,
        out_shape=jax.ShapeDtypeStruct(x.shape, x.dtype),
        grid_spec=pltpu.PrefetchScalarGridSpec(
            num_scalar_prefetch=1,
            grid=(x.shape[0],),
            in_specs=[pl.BlockSpec(block, lambda i, order: (order[i], 0, 0))],
            out_specs=pl.BlockSpec(block, lambda i, order: (i, 0, 0)),
        ),
        name="reorder",
    )(order, x)


def unpack_kernel(x, out):
    places = x.shape[0]
    step = out.shape[0] // places
    for i in range(places):
        base = i * step
        out[base : base + step, :LANES] = x[i, 0, :step, :]
        out[base : base + step // 2, LANES:] = x[i, 0, step:, :HALF]
        out[base + step // 2 : base + step, LANES:] = x[i, 0, step:, HALF:]


def unpack(x, width, cols):
    places, groups, piece_rows, _ = x.shape
    return pl.pallas_call(
        unpack_kernel,
        out_shape=jax.ShapeDtypeStruct((width, cols), BF16),
        grid=(groups,),
        in_specs=[pl.BlockSpec((places, 1, piece_rows, LANES), lambda g: (0, g, 0, 0))],
        out_specs=pl.BlockSpec((width // groups, cols), lambda g: (g, 0)),
        name="unpack",
    )(x)


def dense(tokens, cotangent, route_ids, route_gates, gate_up, down, moment1, moment2, placement):
    experts = lax.axis_size("expert")
    groups = lax.axis_size("dp")
    width = tokens.shape[1]
    units = down.shape[2]
    block = width // groups
    place = jnp.stack([lax.axis_index("expert"), lax.axis_index("dp")]).astype(jnp.int32)

    sent = pack_rows(place, tokens, cotangent, route_ids, route_gates, groups)
    own_weights, *sent_weights = pack_weights(place, gate_up[0], groups)
    blocks = [sent[0]] + [partner(sent[k], "dp", k) for k in range(1, groups)]
    weights = [own_weights] + [
        partner(sent_weights[k - 1], "dp", k) for k in range(1, groups)
    ]
    plane = order_groups(place, blocks)
    chips = [plane] + [partner(plane, "expert", k) for k in range(2, experts, 2)]
    pieces = chips + [partner(x, "expert", 1) for x in chips]

    own_hidden = hidden_blocks(place, pieces, weights, width)
    scaled = scaled_rows(place, pieces, width, block)
    hidden = [own_hidden] + [partner(own_hidden, "dp", k) for k in range(1, groups)]
    packed = update_pieces(place, hidden, scaled, down[0], moment1[0], moment2[0], experts)
    spread = lax.all_to_all(packed, ("expert", "dp"), 0, 0, tiled=True)
    piece_rows = spread.shape[1]
    picked = reorder(placement, spread.reshape(experts, groups * piece_rows, LANES))
    landed = lax.all_to_all(picked, "expert", 0, 0, tiled=True)
    out = unpack(landed.reshape(experts, groups, piece_rows, LANES), width, units // groups)
    return out[None]


def shards(tokens, cotangent, route_ids, *rest):
    every = route_ids.shape[1] == lax.axis_size("expert")
    return (dense if every else routed)(tokens, cotangent, route_ids, *rest)


def solution(mesh):
    placed = (
        P(("expert", "dp"), None),
        P(("expert", "dp"), None),
        P(("expert", "dp"), None),
        P(("expert", "dp"), None),
        P("expert", "dp", None),
        P("expert", "dp", None),
        P("expert", "dp", None),
        P("expert", "dp", None),
        P(),
    )
    return jax.shard_map(
        shards, mesh=mesh, in_specs=placed, out_specs=P("expert", None, "dp"), check_vma=False
    )
```

```python
import functools

import jax
import jax.numpy as jnp
from jax import lax
from jax.experimental import pallas as pl
from jax.experimental.pallas import tpu as pltpu
from jax.sharding import PartitionSpec as P

OPT_STEP = 2


BETA_ONE = 0.9
BETA_TWO = 0.95
ADAM_EPS = 1e-08
LEARN_RATE = 0.25

BF16 = jnp.bfloat16
F32 = jnp.float32
LANES = 128
HALF = LANES // 2
VMEM_BYTES = 48 * 1024 * 1024


def adam(down, moment1, moment2, grad):
    correct_one = 1.0 - BETA_ONE**OPT_STEP
    correct_two = 1.0 - BETA_TWO**OPT_STEP
    first = BETA_ONE * moment1.astype(F32) + (1.0 - BETA_ONE) * grad
    second = BETA_TWO * moment2.astype(F32) + (1.0 - BETA_TWO) * grad * grad
    direction = first / correct_one / (jnp.sqrt(second / correct_two) + ADAM_EPS)
    return (down.astype(F32) - LEARN_RATE * direction).astype(BF16)


def routed(tokens, cotangent, route_ids, route_gates, gate_up, down, moment1, moment2, placement):
    experts = lax.axis_size("expert")
    tok_rows = tokens.shape[0]
    width = tokens.shape[1]
    top_count = route_ids.shape[1]
    hidden_units = down.shape[2]
    capacity = min(tok_rows, 2 * tok_rows * top_count // experts)
    total_slots = experts * capacity
    route_hits = jnp.sum(
        (route_ids[:, :, None] == jnp.arange(experts, dtype=jnp.int32)).astype(jnp.int32), axis=1
    )
    earlier_hits = jnp.cumsum(route_hits, axis=0) - route_hits
    slot_index = jnp.take_along_axis(earlier_hits, route_ids, axis=1)
    target_slot = route_ids * capacity + slot_index
    matched = (target_slot[:, :, None] == jnp.arange(total_slots, dtype=jnp.int32)).astype(F32)
    picker = jnp.sum(matched, axis=1).astype(BF16)
    contract_rows = (((0,), (0,)), ((), ()))
    send_rows = lax.dot_general(picker, tokens, contract_rows, preferred_element_type=F32)
    send_rows = send_rows.astype(BF16).reshape(experts, capacity, width)
    send_grads = lax.dot_general(picker, cotangent, contract_rows, preferred_element_type=F32)
    send_grads = send_grads.astype(BF16).reshape(experts, capacity, width)
    send_gates = jnp.sum(matched * route_gates.astype(F32)[:, :, None], axis=(0, 1))
    send_gates = send_gates.astype(BF16).reshape(experts, capacity)
    rows_in, grads_in, gates_in = (
        lax.all_to_all(send_rows, "expert", split_axis=0, concat_axis=0, tiled=True),
        lax.all_to_all(send_grads, "expert", split_axis=0, concat_axis=0, tiled=True),
        lax.all_to_all(send_gates, "expert", split_axis=0, concat_axis=0, tiled=True),
    )
    pre_all = jnp.dot(
        rows_in.reshape(total_slots, width),
        lax.all_gather(gate_up, "dp", axis=1, tiled=True)[0],
        preferred_element_type=F32,
    )
    hidden = (jax.nn.silu(pre_all[:, :hidden_units]) * pre_all[:, hidden_units:]).astype(BF16)
    scaled = gates_in.reshape(total_slots, 1).astype(F32) * grads_in.reshape(
        total_slots, width
    ).astype(F32)
    partial = lax.dot_general(
        scaled.astype(BF16), hidden, contract_rows, preferred_element_type=F32
    ).astype(BF16)
    grad_share = lax.psum_scatter(partial, "dp", scatter_dimension=0, tiled=True).astype(F32)
    updated = adam(down[0], moment1[0], moment2[0], grad_share)
    column_block = lax.all_to_all(updated, "dp", split_axis=1, concat_axis=0, tiled=True)
    block_cols = column_block.shape[1]
    piece_flat = column_block.reshape(experts, width * block_cols // experts)
    spread = lax.all_to_all(piece_flat, "expert", split_axis=0, concat_axis=0, tiled=True)
    picked = jnp.take(spread, placement, axis=0)
    landed = lax.all_to_all(picked, "expert", split_axis=0, concat_axis=0, tiled=True)
    return landed.reshape(1, width, block_cols)


def partner(x, axis, flip):
    size = lax.axis_size(axis)
    return lax.ppermute(x, axis, [(i, i ^ flip) for i in range(size)])


def smem():
    return pl.BlockSpec(memory_space=pltpu.SMEM)


def whole():
    return pl.BlockSpec(memory_space=pltpu.VMEM)


def pack_rows_kernel(place, tok, cot, ids, gates, *outs):
    groups = len(outs)
    width = tok.shape[1]
    block = width // groups
    group = place[1]
    named = ids[...]
    weights = gates[...].astype(F32)
    expert = lax.broadcasted_iota(jnp.int32, (LANES, named.shape[1]), 0)
    table = jnp.zeros(expert.shape, F32)
    for k in range(named.shape[0]):
        table = table + jnp.where(expert == named[k : k + 1, :], weights[k : k + 1, :], 0.0)
    table = table.T.astype(BF16)
    for flip, out in enumerate(outs):
        start = pl.multiple_of((group ^ flip) * block, LANES)
        out[:, :width] = tok[...]
        out[:, width : width + block] = cot[:, pl.ds(start, block)]
        out[:, width + block :] = table


def pack_rows(place, tokens, cotangent, ids, gates, groups):
    rows, width = tokens.shape
    return pl.pallas_call(
        pack_rows_kernel,
        out_shape=[pltpu.VMEM((rows, width + width // groups + LANES), BF16)] * groups,
        in_specs=[smem()] + [whole()] * 4,
        name="pack_rows",
    )(place, tokens, cotangent, ids.T, gates.T)


def swap_halves(x):
    return jnp.concatenate([x[:, HALF:], x[:, :HALF]], axis=1)


def low_half(shape):
    return lax.broadcasted_iota(jnp.int32, shape, 1) < HALF


def pack_weights_kernel(parts, place, weights, *outs):
    groups = len(parts)
    hidden_units = weights.shape[1] // 2
    group = place[1]

    def write(flip, start, value):
        first = sum(parts[:flip])
        rows = value.shape[0] // parts[flip]
        for i in range(parts[flip]):
            outs[first + i][:, start : start + LANES] = value[i * rows : (i + 1) * rows]

    for pair in range(groups // 2):
        start = (groups + pair) * LANES
        gate = weights[:, start : start + LANES]
        up = swap_halves(weights[:, hidden_units + start : hidden_units + start + LANES])
        low = low_half(gate.shape)
        even, odd = jnp.where(low, gate, up), jnp.where(low, up, gate)
        for flip in range(groups):

            @pl.when((group ^ flip) == 2 * pair)
            def _():
                write(flip, 2 * LANES, even)

            @pl.when((group ^ flip) == 2 * pair + 1)
            def _():
                write(flip, 2 * LANES, odd)

    for flip in range(groups):
        start = pl.multiple_of((group ^ flip) * LANES, LANES)
        write(flip, 0, weights[:, pl.ds(start, LANES)])
        start = pl.multiple_of(hidden_units + start, LANES)
        write(flip, LANES, weights[:, pl.ds(start, LANES)])


def pack_weights(place, weights, parts):
    rows, cols = weights.shape
    outs = [pltpu.VMEM((rows // n, cols // len(parts)), BF16) for n in parts for _ in range(n)]
    return pl.pallas_call(
        functools.partial(pack_weights_kernel, parts),
        out_shape=outs,
        in_specs=[smem(), whole()],
        compiler_params=pltpu.CompilerParams(vmem_limit_bytes=VMEM_BYTES),
        name="pack_weights",
    )(place, weights)


def after(x, *others):
    return lax.optimization_barrier((x, *others))[0]


def in_vmem(x):
    return pltpu.with_memory_space_constraint(x, pltpu.VMEM)


def order_groups_kernel(place, *refs):
    *blocks, out = refs
    for flip, block in enumerate(blocks):
        out[pl.ds(place[1] ^ flip, 1)] = block[...][None]


def order_groups(place, blocks):
    rows, width = blocks[0].shape
    out = pl.pallas_call(
        order_groups_kernel,
        out_shape=pltpu.VMEM((len(blocks), rows, width), BF16),
        in_specs=[smem()] + [whole()] * len(blocks),
        name="order_groups",
    )(place, *[in_vmem(x) for x in blocks])
    return out.reshape(len(blocks) * rows, width)


def hidden_kernel(groups, pieces, spans, place, *refs):
    row_refs, weight_refs, out, toks = refs[:pieces], refs[pieces:-2], refs[-2], refs[-1]
    rows, width = row_refs[0].shape
    block = width // groups
    total = pieces * rows
    for i, ref in enumerate(row_refs):
        toks[i * rows : (i + 1) * rows, :] = ref[...]
    pre = None
    for (flip, first), ref in zip(spans, weight_refs, strict=True):
        start = pl.multiple_of((place[1] ^ flip) * block + first, LANES)
        depth = ref.shape[0]
        term = jnp.dot(toks[:, pl.ds(start, depth)], ref[...], preferred_element_type=F32)
        pre = term if pre is None else pre + term
    gate, up = pre[:, :LANES], pre[:, LANES : 2 * LANES]
    out[:total, :] = (gate / (1.0 + jnp.exp(-gate)) * up).astype(BF16)
    shared = pre[:, 2 * LANES :]
    narrow = shared / (1.0 + jnp.exp(-shared)) * swap_halves(shared)
    low = low_half((total // 2, LANES))
    top, bottom = narrow[: total // 2], swap_halves(narrow[total // 2 :])
    even = lax.rem(place[1], 2) == 0

    @pl.when(even)
    def _():
        out[total:, :] = jnp.where(low, top, bottom).astype(BF16)

    @pl.when(jnp.logical_not(even))
    def _():
        out[total:, :] = jnp.where(low, bottom, top).astype(BF16)


def hidden_blocks(place, pieces, weights, spans, width, groups):
    rows = pieces[0].shape[0]
    total = rows * len(pieces)
    return pl.pallas_call(
        functools.partial(hidden_kernel, groups, len(pieces), spans),
        out_shape=pltpu.VMEM((total + total // 2, LANES), BF16),
        grid=(1,),
        in_specs=[smem()]
        + [pl.BlockSpec((rows, width), lambda i: (0, 0))] * len(pieces)
        + [pl.BlockSpec(x.shape, lambda i: (0, 0)) for x in weights],
        out_specs=pl.BlockSpec((total + total // 2, LANES), lambda i: (0, 0)),
        scratch_shapes=[pltpu.VMEM((total, width), BF16)],
        compiler_params=pltpu.CompilerParams(vmem_limit_bytes=VMEM_BYTES),
        name="hidden_blocks",
    )(place, *[in_vmem(x) for x in [*pieces, *weights]])


def scaled_kernel(pieces, place, *refs):
    cot_refs, gate_refs, out = refs[:pieces], refs[pieces:-1], refs[-1]
    blocks = []
    for cot, table in zip(cot_refs, gate_refs, strict=True):
        gates = table[...].astype(F32)
        lane = lax.broadcasted_iota(jnp.int32, gates.shape, 1)
        gate = jnp.sum(jnp.where(lane == place[0], gates, 0.0), axis=1, keepdims=True)
        blocks.append((gate * cot[...].astype(F32)).astype(BF16))
    out[...] = jnp.concatenate(blocks, axis=0).T


def scaled_rows(place, pieces, width, block):
    rows = pieces[0].shape[0]
    total = rows * len(pieces)
    return pl.pallas_call(
        functools.partial(scaled_kernel, len(pieces)),
        out_shape=jax.ShapeDtypeStruct((block, total), BF16),
        grid=(1,),
        in_specs=[smem()]
        + [pl.BlockSpec((rows, block), lambda i: (0, width // block))] * len(pieces)
        + [pl.BlockSpec((rows, LANES), lambda i: (0, (width + block) // LANES))] * len(pieces),
        out_specs=pl.BlockSpec((block, total), lambda i: (0, 0)),
        compiler_params=pltpu.CompilerParams(vmem_limit_bytes=VMEM_BYTES),
        name="scaled_rows",
    )(place, *pieces, *pieces)


def update_kernel(groups, place, *refs):
    hid_refs, (scaled, down, first, second, out, hidden) = refs[:groups], refs[groups:]
    total = scaled.shape[1]
    units = down.shape[1]

    @pl.when(pl.program_id(0) == 0)
    def _():
        for own in range(groups):

            @pl.when(place[1] == own)
            def _():
                for col in range(groups):
                    hidden[:, col * LANES : (col + 1) * LANES] = hid_refs[own ^ col][:total, :]
                for col in range(0, groups, 2):
                    even, odd = hid_refs[own ^ col][total:, :], hid_refs[own ^ col ^ 1][total:, :]
                    low = low_half(even.shape)
                    start = (groups + col // 2) * LANES
                    hidden[: total // 2, start : start + LANES] = jnp.where(low, even, odd)
                    hidden[total // 2 :, start : start + LANES] = swap_halves(
                        jnp.where(low, odd, even)
                    )

    grad = jnp.dot(scaled[...], hidden[...], preferred_element_type=F32)
    updated = adam(down[...], first[...], second[...], grad).T
    cols = units // groups
    rows = out.shape[1]
    for i in range(out.shape[0] // groups):
        for col in range(groups):
            start = col * cols + i * rows
            out[i * groups + col] = updated[start : start + rows]


def update_pieces(place, hidden, scaled, down, first, second, experts):
    groups = len(hidden)
    features, total = scaled.shape
    units = down.shape[1]
    steps = features // LANES
    places = experts // steps
    piece_rows = units // groups // places
    return pl.pallas_call(
        functools.partial(update_kernel, groups),
        out_shape=jax.ShapeDtypeStruct((experts * groups, piece_rows, LANES), BF16),
        grid=(steps,),
        in_specs=[smem()]
        + [pl.BlockSpec(hidden[0].shape, lambda i: (0, 0))] * groups
        + [pl.BlockSpec((LANES, total), lambda i: (i, 0))]
        + [pl.BlockSpec((LANES, units), lambda i: (i, 0))] * 3,
        out_specs=pl.BlockSpec((places * groups, piece_rows, LANES), lambda i: (i, 0, 0)),
        scratch_shapes=[pltpu.VMEM((total, units), BF16)],
        compiler_params=pltpu.CompilerParams(vmem_limit_bytes=VMEM_BYTES),
        name="update_pieces",
    )(place, *hidden, scaled, down, first, second)


def pick_kernel(place, order, pieces, *outs):
    for flip, out in enumerate(outs):
        out[...] = pieces[order[place[0] ^ flip]]


def pick(place, order, pieces):
    experts = pieces.shape[0]
    return pl.pallas_call(
        pick_kernel,
        out_shape=[pltpu.VMEM(pieces.shape[1:], pieces.dtype)] * experts,
        in_specs=[smem(), smem(), whole()],
        out_specs=[whole()] * experts,
        name="pick",
    )(place, order, pieces)


def unpack_kernel(place, *refs):
    *pieces, out = refs
    groups, rows, _ = pieces[0].shape
    halves = out.shape[1] // rows
    block = out.shape[2] // groups
    for flip, piece in enumerate(pieces):
        spot = place[0] ^ flip
        top = pl.multiple_of((spot % halves) * rows, 16)
        for group in range(groups):
            left = pl.multiple_of(group * block + (spot // halves) * LANES, LANES)
            out[0, pl.ds(top, rows), pl.ds(left, LANES)] = piece[group]


def unpack(place, pieces, width, cols):
    return pl.pallas_call(
        unpack_kernel,
        out_shape=jax.ShapeDtypeStruct((1, cols, width), BF16),
        in_specs=[smem()] + [whole()] * len(pieces),
        out_specs=whole(),
        name="unpack",
    )(place, *[in_vmem(x) for x in pieces])


def dense(tokens, cotangent, route_ids, route_gates, gate_up, down, moment1, moment2, placement):
    experts = lax.axis_size("expert")
    groups = lax.axis_size("dp")
    width = tokens.shape[1]
    units = down.shape[2]
    block = width // groups
    place = jnp.stack([lax.axis_index("expert"), lax.axis_index("dp")]).astype(jnp.int32)

    parts = (1, 1, 1, 1)
    own, near, far, farthest = pack_weights(place, gate_up[0], parts)
    sent = pack_rows(place, tokens, cotangent, route_ids, route_gates, groups)
    blocks = [sent[0]] + [partner(sent[k], "dp", k) for k in range(1, groups)]
    far = partner(after(far, blocks[1]), "dp", 2)
    weights = [own, partner(after(near, far), "dp", 1), far, partner(after(farthest, far), "dp", 3)]
    spans = [(flip, i * (block // n)) for flip, n in enumerate(parts) for i in range(n)]
    plane = order_groups(place, blocks)
    chips = [plane] + [partner(plane, "expert", k) for k in range(2, experts, 2)]
    pieces = chips + [partner(x, "expert", 1) for x in chips]

    own_hidden = hidden_blocks(place, pieces, weights, spans, width, groups)
    scaled = scaled_rows(place, pieces, width, block)
    hidden = [own_hidden] + [partner(own_hidden, "dp", k) for k in range(1, groups)]
    moved = update_pieces(place, hidden, scaled, down[0], moment1[0], moment2[0], experts)
    spread = lax.all_to_all(moved, ("expert", "dp"), 0, 0, tiled=True)
    picked = pick(place, placement, spread.reshape(experts, groups, *spread.shape[1:]))
    landed = [picked[0]] + [partner(picked[k], "expert", k) for k in range(1, experts)]
    return unpack(place, landed, width, units // groups).transpose(0, 2, 1)


def shards(tokens, cotangent, route_ids, *rest):
    every = route_ids.shape[1] == lax.axis_size("expert")
    return (dense if every else routed)(tokens, cotangent, route_ids, *rest)


def solution(mesh):
    placed = (
        P(("expert", "dp"), None),
        P(("expert", "dp"), None),
        P(("expert", "dp"), None),
        P(("expert", "dp"), None),
        P("expert", "dp", None),
        P("expert", "dp", None),
        P("expert", "dp", None),
        P("expert", "dp", None),
        P(),
    )
    return jax.shard_map(
        shards, mesh=mesh, in_specs=placed, out_specs=P("expert", None, "dp"), check_vma=False
    )
```

```python
import functools

import jax
import jax.numpy as jnp
from jax import lax
from jax.experimental import pallas as pl
from jax.experimental.pallas import tpu as pltpu
from jax.sharding import PartitionSpec as P

OPT_STEP = 2


BETA_ONE = 0.9
BETA_TWO = 0.95
ADAM_EPS = 1e-08
LEARN_RATE = 0.25

BF16 = jnp.bfloat16
F32 = jnp.float32
LANES = 128
HALF = LANES // 2
VMEM_BYTES = 48 * 1024 * 1024


def adam(down, moment1, moment2, grad):
    correct_one = 1.0 - BETA_ONE**OPT_STEP
    correct_two = 1.0 - BETA_TWO**OPT_STEP
    first = BETA_ONE * moment1.astype(F32) + (1.0 - BETA_ONE) * grad
    second = BETA_TWO * moment2.astype(F32) + (1.0 - BETA_TWO) * grad * grad
    direction = first / correct_one / (jnp.sqrt(second / correct_two) + ADAM_EPS)
    return (down.astype(F32) - LEARN_RATE * direction).astype(BF16)


def routed(tokens, cotangent, route_ids, route_gates, gate_up, down, moment1, moment2, placement):
    experts = lax.axis_size("expert")
    tok_rows = tokens.shape[0]
    width = tokens.shape[1]
    top_count = route_ids.shape[1]
    hidden_units = down.shape[2]
    capacity = min(tok_rows, 2 * tok_rows * top_count // experts)
    total_slots = experts * capacity
    route_hits = jnp.sum(
        (route_ids[:, :, None] == jnp.arange(experts, dtype=jnp.int32)).astype(jnp.int32), axis=1
    )
    earlier_hits = jnp.cumsum(route_hits, axis=0) - route_hits
    slot_index = jnp.take_along_axis(earlier_hits, route_ids, axis=1)
    target_slot = route_ids * capacity + slot_index
    matched = (target_slot[:, :, None] == jnp.arange(total_slots, dtype=jnp.int32)).astype(F32)
    picker = jnp.sum(matched, axis=1).astype(BF16)
    contract_rows = (((0,), (0,)), ((), ()))
    send_rows = lax.dot_general(picker, tokens, contract_rows, preferred_element_type=F32)
    send_rows = send_rows.astype(BF16).reshape(experts, capacity, width)
    send_grads = lax.dot_general(picker, cotangent, contract_rows, preferred_element_type=F32)
    send_grads = send_grads.astype(BF16).reshape(experts, capacity, width)
    send_gates = jnp.sum(matched * route_gates.astype(F32)[:, :, None], axis=(0, 1))
    send_gates = send_gates.astype(BF16).reshape(experts, capacity)
    rows_in, grads_in, gates_in = (
        lax.all_to_all(send_rows, "expert", split_axis=0, concat_axis=0, tiled=True),
        lax.all_to_all(send_grads, "expert", split_axis=0, concat_axis=0, tiled=True),
        lax.all_to_all(send_gates, "expert", split_axis=0, concat_axis=0, tiled=True),
    )
    pre_all = jnp.dot(
        rows_in.reshape(total_slots, width),
        lax.all_gather(gate_up, "dp", axis=1, tiled=True)[0],
        preferred_element_type=F32,
    )
    hidden = (jax.nn.silu(pre_all[:, :hidden_units]) * pre_all[:, hidden_units:]).astype(BF16)
    scaled = gates_in.reshape(total_slots, 1).astype(F32) * grads_in.reshape(
        total_slots, width
    ).astype(F32)
    partial = lax.dot_general(
        scaled.astype(BF16), hidden, contract_rows, preferred_element_type=F32
    ).astype(BF16)
    grad_share = lax.psum_scatter(partial, "dp", scatter_dimension=0, tiled=True).astype(F32)
    updated = adam(down[0], moment1[0], moment2[0], grad_share)
    column_block = lax.all_to_all(updated, "dp", split_axis=1, concat_axis=0, tiled=True)
    block_cols = column_block.shape[1]
    piece_flat = column_block.reshape(experts, width * block_cols // experts)
    spread = lax.all_to_all(piece_flat, "expert", split_axis=0, concat_axis=0, tiled=True)
    picked = jnp.take(spread, placement, axis=0)
    landed = lax.all_to_all(picked, "expert", split_axis=0, concat_axis=0, tiled=True)
    return landed.reshape(1, width, block_cols)


def partner(x, axis, flip):
    size = lax.axis_size(axis)
    return lax.ppermute(x, axis, [(i, i ^ flip) for i in range(size)])


def smem():
    return pl.BlockSpec(memory_space=pltpu.SMEM)


def whole():
    return pl.BlockSpec(memory_space=pltpu.VMEM)


def pack_rows_kernel(tok, cot, ids, gates, *outs):
    groups = len(outs)
    width = tok.shape[1]
    block = width // groups
    group = lax.axis_index("dp")
    named = ids[...]
    weights = gates[...].astype(F32)
    expert = lax.broadcasted_iota(jnp.int32, (LANES, named.shape[1]), 0)
    table = jnp.zeros(expert.shape, F32)
    for k in range(named.shape[0]):
        table = table + jnp.where(expert == named[k : k + 1, :], weights[k : k + 1, :], 0.0)
    table = table.T.astype(BF16)
    for flip, out in enumerate(outs):
        start = pl.multiple_of((group ^ flip) * block, LANES)
        out[:, :width] = tok[...]
        out[:, width : width + block] = cot[:, pl.ds(start, block)]
        out[:, width + block :] = table


def pack_rows(tokens, cotangent, ids, gates, groups):
    rows, width = tokens.shape
    return pl.pallas_call(
        pack_rows_kernel,
        out_shape=[pltpu.VMEM((rows, width + width // groups + LANES), BF16)] * groups,
        in_specs=[whole()] * 4,
        name="pack_rows",
    )(tokens, cotangent, ids.T, gates.T)


def swap_halves(x):
    return jnp.concatenate([x[:, HALF:], x[:, :HALF]], axis=1)


def low_half(shape):
    return lax.broadcasted_iota(jnp.int32, shape, 1) < HALF


def pack_weights_kernel(parts, weights, *outs):
    groups = len(parts)
    hidden_units = weights.shape[1] // 2
    group = lax.axis_index("dp")

    def write(flip, start, value):
        first = sum(parts[:flip])
        rows = value.shape[0] // parts[flip]
        for i in range(parts[flip]):
            outs[first + i][:, start : start + LANES] = value[i * rows : (i + 1) * rows]

    for pair in range(groups // 2):
        start = (groups + pair) * LANES
        gate = weights[:, start : start + LANES]
        up = swap_halves(weights[:, hidden_units + start : hidden_units + start + LANES])
        low = low_half(gate.shape)
        even, odd = jnp.where(low, gate, up), jnp.where(low, up, gate)
        for flip in range(groups):

            @pl.when((group ^ flip) == 2 * pair)
            def _():
                write(flip, 2 * LANES, even)

            @pl.when((group ^ flip) == 2 * pair + 1)
            def _():
                write(flip, 2 * LANES, odd)

    for flip in range(groups):
        start = pl.multiple_of((group ^ flip) * LANES, LANES)
        write(flip, 0, weights[:, pl.ds(start, LANES)])
        start = pl.multiple_of(hidden_units + start, LANES)
        write(flip, LANES, weights[:, pl.ds(start, LANES)])


def pack_weights(weights, parts):
    rows, cols = weights.shape
    outs = [pltpu.VMEM((rows // n, cols // len(parts)), BF16) for n in parts for _ in range(n)]
    return pl.pallas_call(
        functools.partial(pack_weights_kernel, parts),
        out_shape=outs,
        in_specs=[whole()],
        compiler_params=pltpu.CompilerParams(vmem_limit_bytes=VMEM_BYTES),
        name="pack_weights",
    )(weights)


def after(x, *others):
    return lax.optimization_barrier((x, *others))[0]


def in_vmem(x):
    return pltpu.with_memory_space_constraint(x, pltpu.VMEM)


def order_groups_kernel(*refs):
    *blocks, out = refs
    for flip, block in enumerate(blocks):
        out[pl.ds(lax.axis_index("dp") ^ flip, 1)] = block[...][None]


def order_groups(blocks):
    rows, width = blocks[0].shape
    out = pl.pallas_call(
        order_groups_kernel,
        out_shape=pltpu.VMEM((len(blocks), rows, width), BF16),
        in_specs=[whole()] * len(blocks),
        name="order_groups",
    )(*[in_vmem(x) for x in blocks])
    return out.reshape(len(blocks) * rows, width)


def hidden_kernel(groups, pieces, spans, *refs):
    row_refs, weight_refs, out, toks = refs[:pieces], refs[pieces:-2], refs[-2], refs[-1]
    rows, width = row_refs[0].shape
    block = width // groups
    total = pieces * rows
    for i, ref in enumerate(row_refs):
        toks[i * rows : (i + 1) * rows, :] = ref[...]
    pre = None
    for (flip, first), ref in zip(spans, weight_refs, strict=True):
        start = pl.multiple_of((lax.axis_index("dp") ^ flip) * block + first, LANES)
        depth = ref.shape[0]
        term = jnp.dot(toks[:, pl.ds(start, depth)], ref[...], preferred_element_type=F32)
        pre = term if pre is None else pre + term
    gate, up = pre[:, :LANES], pre[:, LANES : 2 * LANES]
    out[:total, :] = (gate / (1.0 + jnp.exp(-gate)) * up).astype(BF16)
    shared = pre[:, 2 * LANES :]
    narrow = shared / (1.0 + jnp.exp(-shared)) * swap_halves(shared)
    low = low_half((total // 2, LANES))
    top, bottom = narrow[: total // 2], swap_halves(narrow[total // 2 :])
    even = lax.rem(lax.axis_index("dp"), 2) == 0

    @pl.when(even)
    def _():
        out[total:, :] = jnp.where(low, top, bottom).astype(BF16)

    @pl.when(jnp.logical_not(even))
    def _():
        out[total:, :] = jnp.where(low, bottom, top).astype(BF16)


def hidden_blocks(pieces, weights, spans, width, groups):
    rows = pieces[0].shape[0]
    total = rows * len(pieces)
    return pl.pallas_call(
        functools.partial(hidden_kernel, groups, len(pieces), spans),
        out_shape=pltpu.VMEM((total + total // 2, LANES), BF16),
        grid=(1,),
        in_specs=[pl.BlockSpec((rows, width), lambda i: (0, 0))] * len(pieces)
        + [pl.BlockSpec(x.shape, lambda i: (0, 0)) for x in weights],
        out_specs=pl.BlockSpec((total + total // 2, LANES), lambda i: (0, 0)),
        scratch_shapes=[pltpu.VMEM((total, width), BF16)],
        compiler_params=pltpu.CompilerParams(vmem_limit_bytes=VMEM_BYTES),
        name="hidden_blocks",
    )(*[in_vmem(x) for x in [*pieces, *weights]])


def scaled_kernel(pieces, *refs):
    cot_refs, gate_refs, out = refs[:pieces], refs[pieces:-1], refs[-1]
    blocks = []
    for cot, table in zip(cot_refs, gate_refs, strict=True):
        gates = table[...].astype(F32)
        lane = lax.broadcasted_iota(jnp.int32, gates.shape, 1)
        gate = jnp.sum(jnp.where(lane == lax.axis_index("expert"), gates, 0.0), axis=1, keepdims=True)
        blocks.append((gate * cot[...].astype(F32)).astype(BF16))
    out[...] = jnp.concatenate(blocks, axis=0).T


def scaled_rows(pieces, width, block):
    rows = pieces[0].shape[0]
    total = rows * len(pieces)
    return pl.pallas_call(
        functools.partial(scaled_kernel, len(pieces)),
        out_shape=jax.ShapeDtypeStruct((block, total), BF16),
        grid=(1,),
        in_specs=[pl.BlockSpec((rows, block), lambda i: (0, width // block))] * len(pieces)
        + [pl.BlockSpec((rows, LANES), lambda i: (0, (width + block) // LANES))] * len(pieces),
        out_specs=pl.BlockSpec((block, total), lambda i: (0, 0)),
        compiler_params=pltpu.CompilerParams(vmem_limit_bytes=VMEM_BYTES),
        name="scaled_rows",
    )(*pieces, *pieces)


def update_kernel(groups, *refs):
    hid_refs, (scaled, down, first, second, out, hidden) = refs[:groups], refs[groups:]
    total = scaled.shape[1]
    units = down.shape[1]

    @pl.when(pl.program_id(0) == 0)
    def _():
        for own in range(groups):

            @pl.when(lax.axis_index("dp") == own)
            def _():
                for col in range(groups):
                    hidden[:, col * LANES : (col + 1) * LANES] = hid_refs[own ^ col][:total, :]
                for col in range(0, groups, 2):
                    even, odd = hid_refs[own ^ col][total:, :], hid_refs[own ^ col ^ 1][total:, :]
                    low = low_half(even.shape)
                    start = (groups + col // 2) * LANES
                    hidden[: total // 2, start : start + LANES] = jnp.where(low, even, odd)
                    hidden[total // 2 :, start : start + LANES] = swap_halves(
                        jnp.where(low, odd, even)
                    )

    grad = jnp.dot(scaled[...], hidden[...], preferred_element_type=F32)
    updated = adam(down[...], first[...], second[...], grad).T
    cols = units // groups
    rows = out.shape[1]
    for i in range(out.shape[0] // groups):
        for col in range(groups):
            start = col * cols + i * rows
            out[i * groups + col] = updated[start : start + rows]


def update_pieces(hidden, scaled, down, first, second, experts):
    groups = len(hidden)
    features, total = scaled.shape
    units = down.shape[1]
    steps = features // LANES
    places = experts // steps
    piece_rows = units // groups // places
    return pl.pallas_call(
        functools.partial(update_kernel, groups),
        out_shape=jax.ShapeDtypeStruct((experts * groups, piece_rows, LANES), BF16),
        grid=(steps,),
        in_specs=[pl.BlockSpec(hidden[0].shape, lambda i: (0, 0))] * groups
        + [pl.BlockSpec((LANES, total), lambda i: (i, 0))]
        + [pl.BlockSpec((LANES, units), lambda i: (i, 0))] * 3,
        out_specs=pl.BlockSpec((places * groups, piece_rows, LANES), lambda i: (i, 0, 0)),
        scratch_shapes=[pltpu.VMEM((total, units), BF16)],
        compiler_params=pltpu.CompilerParams(vmem_limit_bytes=VMEM_BYTES),
        name="update_pieces",
    )(*hidden, scaled, down, first, second)


def pick_kernel(order, pieces, *outs):
    for flip, out in enumerate(outs):
        out[...] = pieces[order[lax.axis_index("expert") ^ flip]]


def pick(order, pieces):
    experts = pieces.shape[0]
    return pl.pallas_call(
        pick_kernel,
        out_shape=[pltpu.VMEM(pieces.shape[1:], pieces.dtype)] * experts,
        in_specs=[smem(), whole()],
        out_specs=[whole()] * experts,
        name="pick",
    )(order, pieces)


def unpack_kernel(*refs):
    *pieces, out = refs
    groups, rows, _ = pieces[0].shape
    halves = out.shape[1] // rows
    block = out.shape[2] // groups
    for flip, piece in enumerate(pieces):
        spot = lax.axis_index("expert") ^ flip
        top = pl.multiple_of((spot % halves) * rows, 16)
        for group in range(groups):
            left = pl.multiple_of(group * block + (spot // halves) * LANES, LANES)
            out[0, pl.ds(top, rows), pl.ds(left, LANES)] = piece[group]


def unpack(pieces, width, cols):
    return pl.pallas_call(
        unpack_kernel,
        out_shape=jax.ShapeDtypeStruct((1, cols, width), BF16),
        in_specs=[whole()] * len(pieces),
        out_specs=whole(),
        name="unpack",
    )(*[in_vmem(x) for x in pieces])


def dense(tokens, cotangent, route_ids, route_gates, gate_up, down, moment1, moment2, placement):
    experts = lax.axis_size("expert")
    groups = lax.axis_size("dp")
    width = tokens.shape[1]
    units = down.shape[2]
    block = width // groups

    parts = (1, 1, 1, 1)
    own, near, far, farthest = pack_weights(gate_up[0], parts)
    sent = pack_rows(tokens, cotangent, route_ids, route_gates, groups)
    blocks = [sent[0]] + [partner(sent[k], "dp", k) for k in range(1, groups)]
    spans = [(flip, i * (block // n)) for flip, n in enumerate(parts) for i in range(n)]
    plane = order_groups(blocks)
    chips = [plane] + [partner(plane, "expert", k) for k in range(2, experts, 2)]
    pieces = chips + [partner(x, "expert", 1) for x in chips]
    far = partner(after(far, blocks[1]), "dp", 2)
    near = partner(after(near, chips[1]), "dp", 1)
    farthest = partner(after(farthest, far), "dp", 3)
    weights = [own, near, far, farthest]

    own_hidden = hidden_blocks(pieces, weights, spans, width, groups)
    scaled = scaled_rows(pieces, width, block)
    hidden = [own_hidden] + [partner(own_hidden, "dp", k) for k in range(1, groups)]
    moved = update_pieces(hidden, scaled, down[0], moment1[0], moment2[0], experts)
    spread = lax.all_to_all(moved, ("expert", "dp"), 0, 0, tiled=True)
    picked = pick(placement, spread.reshape(experts, groups, *spread.shape[1:]))
    landed = [picked[0]] + [partner(picked[k], "expert", k) for k in range(1, experts)]
    return unpack(landed, width, units // groups).transpose(0, 2, 1)


def shards(tokens, cotangent, route_ids, *rest):
    every = route_ids.shape[1] == lax.axis_size("expert")
    return (dense if every else routed)(tokens, cotangent, route_ids, *rest)


def solution(mesh):
    placed = (
        P(("expert", "dp"), None),
        P(("expert", "dp"), None),
        P(("expert", "dp"), None),
        P(("expert", "dp"), None),
        P("expert", "dp", None),
        P("expert", "dp", None),
        P("expert", "dp", None),
        P("expert", "dp", None),
        P(),
    )
    return jax.shard_map(
        shards, mesh=mesh, in_specs=placed, out_specs=P("expert", None, "dp"), check_vma=False
    )
```

```python
import functools

import jax
import jax.numpy as jnp
from jax import lax
from jax.experimental import pallas as pl
from jax.experimental.pallas import tpu as pltpu
from jax.sharding import PartitionSpec as P

OPT_STEP = 2


BETA_ONE = 0.9
BETA_TWO = 0.95
ADAM_EPS = 1e-08
LEARN_RATE = 0.25

BF16 = jnp.bfloat16
F32 = jnp.float32
LANES = 128
HALF = LANES // 2
CORES = 2
VMEM_BYTES = 24 * 1024 * 1024


def adam(down, moment1, moment2, grad):
    correct_one = 1.0 - BETA_ONE**OPT_STEP
    correct_two = 1.0 - BETA_TWO**OPT_STEP
    first = BETA_ONE * moment1.astype(F32) + (1.0 - BETA_ONE) * grad
    second = BETA_TWO * moment2.astype(F32) + (1.0 - BETA_TWO) * grad * grad
    direction = first / correct_one / (jnp.sqrt(second / correct_two) + ADAM_EPS)
    return (down.astype(F32) - LEARN_RATE * direction).astype(BF16)


def routed(tokens, cotangent, route_ids, route_gates, gate_up, down, moment1, moment2, placement):
    experts = lax.axis_size("expert")
    tok_rows = tokens.shape[0]
    width = tokens.shape[1]
    top_count = route_ids.shape[1]
    hidden_units = down.shape[2]
    capacity = min(tok_rows, 2 * tok_rows * top_count // experts)
    total_slots = experts * capacity
    route_hits = jnp.sum(
        (route_ids[:, :, None] == jnp.arange(experts, dtype=jnp.int32)).astype(jnp.int32), axis=1
    )
    earlier_hits = jnp.cumsum(route_hits, axis=0) - route_hits
    slot_index = jnp.take_along_axis(earlier_hits, route_ids, axis=1)
    target_slot = route_ids * capacity + slot_index
    matched = (target_slot[:, :, None] == jnp.arange(total_slots, dtype=jnp.int32)).astype(F32)
    picker = jnp.sum(matched, axis=1).astype(BF16)
    contract_rows = (((0,), (0,)), ((), ()))
    send_rows = lax.dot_general(picker, tokens, contract_rows, preferred_element_type=F32)
    send_rows = send_rows.astype(BF16).reshape(experts, capacity, width)
    send_grads = lax.dot_general(picker, cotangent, contract_rows, preferred_element_type=F32)
    send_grads = send_grads.astype(BF16).reshape(experts, capacity, width)
    send_gates = jnp.sum(matched * route_gates.astype(F32)[:, :, None], axis=(0, 1))
    send_gates = send_gates.astype(BF16).reshape(experts, capacity)
    rows_in, grads_in, gates_in = (
        lax.all_to_all(send_rows, "expert", split_axis=0, concat_axis=0, tiled=True),
        lax.all_to_all(send_grads, "expert", split_axis=0, concat_axis=0, tiled=True),
        lax.all_to_all(send_gates, "expert", split_axis=0, concat_axis=0, tiled=True),
    )
    pre_all = jnp.dot(
        rows_in.reshape(total_slots, width),
        lax.all_gather(gate_up, "dp", axis=1, tiled=True)[0],
        preferred_element_type=F32,
    )
    hidden = (jax.nn.silu(pre_all[:, :hidden_units]) * pre_all[:, hidden_units:]).astype(BF16)
    scaled = gates_in.reshape(total_slots, 1).astype(F32) * grads_in.reshape(
        total_slots, width
    ).astype(F32)
    partial = lax.dot_general(
        scaled.astype(BF16), hidden, contract_rows, preferred_element_type=F32
    ).astype(BF16)
    grad_share = lax.psum_scatter(partial, "dp", scatter_dimension=0, tiled=True).astype(F32)
    updated = adam(down[0], moment1[0], moment2[0], grad_share)
    column_block = lax.all_to_all(updated, "dp", split_axis=1, concat_axis=0, tiled=True)
    block_cols = column_block.shape[1]
    piece_flat = column_block.reshape(experts, width * block_cols // experts)
    spread = lax.all_to_all(piece_flat, "expert", split_axis=0, concat_axis=0, tiled=True)
    picked = jnp.take(spread, placement, axis=0)
    landed = lax.all_to_all(picked, "expert", split_axis=0, concat_axis=0, tiled=True)
    return landed.reshape(1, width, block_cols)


def partner(x, axis, flip):
    size = lax.axis_size(axis)
    return lax.ppermute(x, axis, [(i, i ^ flip) for i in range(size)])


def smem():
    return pl.BlockSpec(memory_space=pltpu.SMEM)


def whole():
    return pl.BlockSpec(memory_space=pltpu.VMEM)


def pack_rows_kernel(tok, cot, ids, gates, *outs):
    groups = len(outs)
    width = tok.shape[1]
    block = width // groups
    group = lax.axis_index("dp")
    named = ids[...]
    weights = gates[...].astype(F32)
    expert = lax.broadcasted_iota(jnp.int32, (LANES, named.shape[1]), 0)
    table = jnp.zeros(expert.shape, F32)
    for k in range(named.shape[0]):
        table = table + jnp.where(expert == named[k : k + 1, :], weights[k : k + 1, :], 0.0)
    table = table.T.astype(BF16)
    for flip, out in enumerate(outs):
        start = pl.multiple_of((group ^ flip) * block, LANES)
        out[:, :width] = tok[...]
        out[:, width : width + block] = cot[:, pl.ds(start, block)]
        out[:, width + block :] = table


def pack_rows(tokens, cotangent, ids, gates, groups):
    rows, width = tokens.shape
    return pl.pallas_call(
        pack_rows_kernel,
        out_shape=[pltpu.VMEM((rows, width + width // groups + LANES), BF16)] * groups,
        in_specs=[whole()] * 4,
        name="pack_rows",
    )(tokens, cotangent, ids.T, gates.T)


def swap_halves(x):
    return jnp.concatenate([x[:, HALF:], x[:, :HALF]], axis=1)


def low_half(shape):
    return lax.broadcasted_iota(jnp.int32, shape, 1) < HALF


def pack_weights_kernel(weights, *outs):
    groups = len(outs)
    hidden_units = weights.shape[1] // 2
    group = lax.axis_index("dp")
    low = low_half((weights.shape[0], LANES))
    for pair in range(groups // 2):
        gate, up = (
            [
                weights[:, start + i * LANES : start + (i + 1) * LANES]
                for i in range(pair * 3, pair * 3 + 3)
            ]
            for start in (0, hidden_units)
        )
        even = gate[0], up[0], jnp.where(low, gate[1], swap_halves(up[1]))
        odd = (
            swap_halves(jnp.where(low, gate[2], gate[1])),
            swap_halves(jnp.where(low, up[2], up[1])),
            jnp.where(low, swap_halves(up[2]), gate[2]),
        )
        for parity, tiles in enumerate((even, odd)):
            for flip, out in enumerate(outs):

                @pl.when((group ^ flip) == 2 * pair + parity)
                def _():
                    for i, tile in enumerate(tiles):
                        out[:, i * LANES : (i + 1) * LANES] = tile


def pack_weights(weights, groups):
    rows, cols = weights.shape
    return pl.pallas_call(
        pack_weights_kernel,
        out_shape=[pltpu.VMEM((rows, cols // groups), BF16)] * groups,
        in_specs=[whole()],
        compiler_params=pltpu.CompilerParams(vmem_limit_bytes=VMEM_BYTES),
        name="pack_weights",
    )(weights)


def after(x, *others):
    return lax.optimization_barrier((x, *others))[0]


def in_vmem(x):
    return pltpu.with_memory_space_constraint(x, pltpu.VMEM)


def order_groups_kernel(*refs):
    *blocks, out = refs
    for flip, block in enumerate(blocks):
        out[pl.ds(lax.axis_index("dp") ^ flip, 1)] = block[...][None]


def order_groups(blocks):
    rows, width = blocks[0].shape
    out = pl.pallas_call(
        order_groups_kernel,
        out_shape=pltpu.VMEM((len(blocks), rows, width), BF16),
        in_specs=[whole()] * len(blocks),
        name="order_groups",
    )(*[in_vmem(x) for x in blocks])
    return out.reshape(len(blocks) * rows, width)


def silu(x):
    return x / (1.0 + jnp.exp(-x))


def hidden_kernel(pieces, bounds, *refs):
    row_refs, refs = refs[:pieces], refs[pieces:]
    groups = lax.axis_size("dp")
    weight_refs, outs, (toks, hidden) = refs[:groups], refs[groups:-2], refs[-2:]
    rows, width = row_refs[0].shape[0], toks.shape[1]
    block = width // groups
    group = lax.axis_index("dp")
    for i, ref in enumerate(row_refs):
        toks[i * rows : (i + 1) * rows, :] = ref[:, :width]
    pre = None
    for flip, ref in enumerate(weight_refs):
        start = pl.multiple_of((group ^ flip) * block, LANES)
        term = jnp.dot(toks[:, pl.ds(start, block)], ref[...], preferred_element_type=F32)
        pre = term if pre is None else pre + term
    gate, up, shared = (pre[:, i * LANES : (i + 1) * LANES] for i in range(3))
    hidden[:LANES, :] = (silu(gate) * up).T.astype(BF16)
    halves = (silu(shared) * swap_halves(shared)).T.astype(BF16)
    for parity in range(2):

        @pl.when(lax.rem(group, 2) == parity)
        def _():
            hidden[LANES:, :] = halves[parity * HALF : (parity + 1) * HALF]

    for (start, end), out in zip(bounds, outs, strict=True):
        out[...] = hidden[start:end, :]


def hidden_units(pieces, weights, width, bounds):
    rows = pieces[0].shape[0]
    total = rows * len(pieces)
    return pl.pallas_call(
        functools.partial(hidden_kernel, len(pieces), bounds),
        out_shape=[pltpu.VMEM((end - start, total), BF16) for start, end in bounds],
        in_specs=[whole()] * (len(pieces) + len(weights)),
        scratch_shapes=[
            pltpu.VMEM((total, width), BF16),
            pltpu.VMEM((weights[0].shape[1] // 2, total), BF16),
        ],
        compiler_params=pltpu.CompilerParams(vmem_limit_bytes=VMEM_BYTES),
        name="hidden_units",
    )(*[in_vmem(x) for x in [*pieces, *weights]])


def scaled_kernel(start, *refs):
    *pieces, out = refs
    rows, block = pieces[0].shape[0], out.shape[1]
    blocks = []
    for piece in pieces:
        gates = piece[:, start + block :].astype(F32)
        lane = lax.broadcasted_iota(jnp.int32, gates.shape, 1)
        here = lane == lax.axis_index("expert")
        gate = jnp.sum(jnp.where(here, gates, 0.0), axis=1, keepdims=True)
        cot = piece[:, start : start + block].astype(F32)
        blocks.append((gate * cot).astype(BF16))
    out[...] = jnp.concatenate(blocks, axis=0)


def scaled_rows(pieces, width, block):
    total = pieces[0].shape[0] * len(pieces)
    return pl.pallas_call(
        functools.partial(scaled_kernel, width),
        out_shape=pltpu.VMEM((total, block), BF16),
        in_specs=[whole()] * len(pieces),
        compiler_params=pltpu.CompilerParams(vmem_limit_bytes=VMEM_BYTES),
        name="scaled_rows",
    )(*[in_vmem(x) for x in pieces])


def flip_kernel(*refs):
    half = len(refs) // 2
    for x, out in zip(refs[:half], refs[half:], strict=True):
        out[...] = x[...].T


def transposed(*arrays):
    return pl.pallas_call(
        flip_kernel,
        out_shape=[pltpu.VMEM(x.shape[::-1], x.dtype) for x in arrays],
        in_specs=[whole()] * len(arrays),
        compiler_params=pltpu.CompilerParams(vmem_limit_bytes=VMEM_BYTES),
        name="transposed",
    )(*arrays)


def update_kernel(start, *refs):
    groups = lax.axis_size("dp")
    hid_refs, (scaled, down, first, second), refs = refs[:groups], refs[groups : groups + 4], refs[groups + 4 :]
    outs, hidden = refs[:-1], refs[-1]
    rows = hid_refs[0].shape[0]
    cols = down.shape[0] // groups
    for flip, ref in enumerate(hid_refs):
        hidden[flip * rows : (flip + 1) * rows, :] = ref[...]
    for flip, out in enumerate(outs):
        tile = (lax.axis_index("expert") // CORES) ^ flip
        lanes = pl.ds(pl.multiple_of(tile * LANES, LANES), LANES)
        grad = jnp.dot(hidden[...], scaled[:, lanes], preferred_element_type=F32)
        for other in range(groups):
            at = pl.multiple_of((lax.axis_index("dp") ^ other) * cols + start, 16)
            here = pl.ds(at, rows), lanes
            part = grad[other * rows : (other + 1) * rows]
            out[other] = adam(down[here], first[here], second[here], part)


def update_tiles(hidden, scaled, state, start, chips):
    groups = len(hidden)
    rows, total = hidden[0].shape
    return pl.pallas_call(
        functools.partial(update_kernel, start),
        out_shape=[pltpu.VMEM((groups, rows, scaled.shape[1] // chips), BF16)] * chips,
        in_specs=[whole()] * (groups + 4),
        scratch_shapes=[pltpu.VMEM((groups * rows, total), BF16)],
        compiler_params=pltpu.CompilerParams(vmem_limit_bytes=VMEM_BYTES),
        name="update_tiles",
    )(*[in_vmem(x) for x in [*hidden, scaled, *state]])


def regroup_kernel(*refs):
    chips = lax.axis_size("expert") // CORES
    tiles, outs = refs[:chips], refs[chips:]
    own = lax.axis_index("expert") // CORES
    for flip, tile in enumerate(tiles):
        for other, out in enumerate(outs):
            out[pl.ds(own ^ flip, 1)] = tile[other][None]


def regroup(tiles):
    groups, *tile = tiles[0].shape
    return pl.pallas_call(
        regroup_kernel,
        out_shape=[pltpu.VMEM((len(tiles), *tile), BF16)] * groups,
        in_specs=[whole()] * len(tiles),
        name="regroup",
    )(*[in_vmem(x) for x in tiles])


def pick_kernel(order, *refs):
    groups, chips = lax.axis_size("dp"), lax.axis_size("expert") // CORES
    kept, swapped, outs = refs[:groups], refs[groups : 2 * groups], refs[2 * groups :]
    spot = lax.axis_index("expert")
    core = lax.rem(spot, CORES)
    for flip, out in enumerate(outs):
        source = order[spot ^ (flip * CORES)]
        chip, here = source // CORES, lax.rem(source, CORES) == core

        @pl.when(here)
        def _():
            for i in range(groups):
                out[i] = kept[i][chip]

        @pl.when(jnp.logical_not(here))
        def _():
            for i in range(groups):
                out[i] = swapped[i][chip]


def pick(order, kept, swapped):
    chips, *tile = kept[0].shape
    return pl.pallas_call(
        pick_kernel,
        out_shape=[pltpu.VMEM((len(kept), *tile), BF16)] * chips,
        in_specs=[smem()] + [whole()] * (2 * len(kept)),
        name="pick",
    )(order, *[in_vmem(x) for x in [*kept, *swapped]])


def unpack_kernel(bounds, *refs):
    *pieces, out = refs
    groups = pieces[0].shape[0]
    block = out.shape[2] // groups
    chips = len(pieces) // len(bounds)
    for i, piece in enumerate(pieces):
        start, end = bounds[i // chips]
        tile = (lax.axis_index("expert") // CORES) ^ (i % chips)
        for other in range(groups):
            left = (lax.axis_index("dp") ^ other) * block + tile * LANES
            out[0, start:end, pl.ds(pl.multiple_of(left, LANES), LANES)] = piece[other]


def unpack(pieces, bounds, width, cols):
    return pl.pallas_call(
        functools.partial(unpack_kernel, bounds),
        out_shape=jax.ShapeDtypeStruct((1, cols, width), BF16),
        in_specs=[whole()] * len(pieces),
        out_specs=whole(),
        name="unpack",
    )(*[in_vmem(x) for x in pieces])


def dense(tokens, cotangent, route_ids, route_gates, gate_up, down, moment1, moment2, placement):
    experts = lax.axis_size("expert")
    groups = lax.axis_size("dp")
    width = tokens.shape[1]
    units = down.shape[2]
    block = width // groups

    own, near, far, farthest = pack_weights(gate_up[0], groups)
    sent = pack_rows(tokens, cotangent, route_ids, route_gates, groups)
    blocks = [sent[0]] + [partner(sent[k], "dp", k) for k in range(1, groups)]
    state = transposed(down[0], moment1[0], moment2[0])
    plane = order_groups([after(blocks[0], state[0]), *blocks[1:]])
    chips = [plane] + [partner(plane, "expert", k) for k in range(2, experts, 2)]
    pieces = chips + [partner(x, "expert", 1) for x in chips]
    far = partner(after(far, blocks[1]), "dp", 2)
    near = partner(after(near, chips[1]), "dp", 1)
    farthest = partner(after(farthest, far), "dp", 3)

    cols = units // groups
    bounds = ((0, cols),)
    parts = hidden_units(pieces, [own, near, far, farthest], width, bounds)
    scaled = scaled_rows(pieces, width, block)
    landed = []
    for (start, _), part in zip(bounds, parts, strict=True):
        hidden = [part] + [partner(part, "dp", k) for k in range(1, groups)]
        tiles = update_tiles(hidden, scaled, state, start, experts // CORES)
        tiles = [tiles[0]] + [
            partner(tiles[k], "expert", k * CORES) for k in range(1, len(tiles))
        ]
        split = regroup(tiles)
        kept = [split[0]] + [partner(split[k], "dp", k) for k in range(1, groups)]
        swapped = [partner(x, "expert", 1) for x in kept]
        picked = pick(placement, kept, swapped)
        landed += [picked[0]] + [
            partner(picked[k], "expert", k * CORES) for k in range(1, len(picked))
        ]
    return unpack(landed, bounds, width, cols).transpose(0, 2, 1)


def shards(tokens, cotangent, route_ids, *rest):
    every = route_ids.shape[1] == lax.axis_size("expert")
    return (dense if every else routed)(tokens, cotangent, route_ids, *rest)


def solution(mesh):
    placed = (
        P(("expert", "dp"), None),
        P(("expert", "dp"), None),
        P(("expert", "dp"), None),
        P(("expert", "dp"), None),
        P("expert", "dp", None),
        P("expert", "dp", None),
        P("expert", "dp", None),
        P("expert", "dp", None),
        P(),
    )
    return jax.shard_map(
        shards, mesh=mesh, in_specs=placed, out_specs=P("expert", None, "dp"), check_vma=False
    )
```

```python
import functools

import jax
import jax.numpy as jnp
from jax import lax
from jax.experimental import pallas as pl
from jax.experimental.pallas import tpu as pltpu
from jax.sharding import PartitionSpec as P

OPT_STEP = 2


BETA_ONE = 0.9
BETA_TWO = 0.95
ADAM_EPS = 1e-08
LEARN_RATE = 0.25

BF16 = jnp.bfloat16
F32 = jnp.float32
LANES = 128
HALF = LANES // 2
CORES = 2
VMEM_BYTES = 24 * 1024 * 1024


def adam(down, moment1, moment2, grad):
    correct_one = 1.0 - BETA_ONE**OPT_STEP
    correct_two = 1.0 - BETA_TWO**OPT_STEP
    first = BETA_ONE * moment1.astype(F32) + (1.0 - BETA_ONE) * grad
    second = BETA_TWO * moment2.astype(F32) + (1.0 - BETA_TWO) * grad * grad
    direction = first / correct_one / (jnp.sqrt(second / correct_two) + ADAM_EPS)
    return (down.astype(F32) - LEARN_RATE * direction).astype(BF16)


def routed(tokens, cotangent, route_ids, route_gates, gate_up, down, moment1, moment2, placement):
    experts = lax.axis_size("expert")
    tok_rows = tokens.shape[0]
    width = tokens.shape[1]
    top_count = route_ids.shape[1]
    hidden_units = down.shape[2]
    capacity = min(tok_rows, 2 * tok_rows * top_count // experts)
    total_slots = experts * capacity
    route_hits = jnp.sum(
        (route_ids[:, :, None] == jnp.arange(experts, dtype=jnp.int32)).astype(jnp.int32), axis=1
    )
    earlier_hits = jnp.cumsum(route_hits, axis=0) - route_hits
    slot_index = jnp.take_along_axis(earlier_hits, route_ids, axis=1)
    target_slot = route_ids * capacity + slot_index
    matched = (target_slot[:, :, None] == jnp.arange(total_slots, dtype=jnp.int32)).astype(F32)
    picker = jnp.sum(matched, axis=1).astype(BF16)
    contract_rows = (((0,), (0,)), ((), ()))
    send_rows = lax.dot_general(picker, tokens, contract_rows, preferred_element_type=F32)
    send_rows = send_rows.astype(BF16).reshape(experts, capacity, width)
    send_grads = lax.dot_general(picker, cotangent, contract_rows, preferred_element_type=F32)
    send_grads = send_grads.astype(BF16).reshape(experts, capacity, width)
    send_gates = jnp.sum(matched * route_gates.astype(F32)[:, :, None], axis=(0, 1))
    send_gates = send_gates.astype(BF16).reshape(experts, capacity)
    rows_in, grads_in, gates_in = (
        lax.all_to_all(send_rows, "expert", split_axis=0, concat_axis=0, tiled=True),
        lax.all_to_all(send_grads, "expert", split_axis=0, concat_axis=0, tiled=True),
        lax.all_to_all(send_gates, "expert", split_axis=0, concat_axis=0, tiled=True),
    )
    pre_all = jnp.dot(
        rows_in.reshape(total_slots, width),
        lax.all_gather(gate_up, "dp", axis=1, tiled=True)[0],
        preferred_element_type=F32,
    )
    hidden = (jax.nn.silu(pre_all[:, :hidden_units]) * pre_all[:, hidden_units:]).astype(BF16)
    scaled = gates_in.reshape(total_slots, 1).astype(F32) * grads_in.reshape(
        total_slots, width
    ).astype(F32)
    partial = lax.dot_general(
        scaled.astype(BF16), hidden, contract_rows, preferred_element_type=F32
    ).astype(BF16)
    grad_share = lax.psum_scatter(partial, "dp", scatter_dimension=0, tiled=True).astype(F32)
    updated = adam(down[0], moment1[0], moment2[0], grad_share)
    column_block = lax.all_to_all(updated, "dp", split_axis=1, concat_axis=0, tiled=True)
    block_cols = column_block.shape[1]
    piece_flat = column_block.reshape(experts, width * block_cols // experts)
    spread = lax.all_to_all(piece_flat, "expert", split_axis=0, concat_axis=0, tiled=True)
    picked = jnp.take(spread, placement, axis=0)
    landed = lax.all_to_all(picked, "expert", split_axis=0, concat_axis=0, tiled=True)
    return landed.reshape(1, width, block_cols)


def partner(x, axis, flip):
    size = lax.axis_size(axis)
    return lax.ppermute(x, axis, [(i, i ^ flip) for i in range(size)])


def smem():
    return pl.BlockSpec(memory_space=pltpu.SMEM)


def whole():
    return pl.BlockSpec(memory_space=pltpu.VMEM)


def pack_rows_kernel(tok, cot, ids, gates, *outs):
    groups = len(outs)
    width = tok.shape[1]
    block = width // groups
    group = lax.axis_index("dp")
    named = ids[...]
    weights = gates[...].astype(F32)
    expert = lax.broadcasted_iota(jnp.int32, (LANES, named.shape[1]), 0)
    table = jnp.zeros(expert.shape, F32)
    for k in range(named.shape[0]):
        table = table + jnp.where(expert == named[k : k + 1, :], weights[k : k + 1, :], 0.0)
    table = table.T.astype(BF16)
    for flip, out in enumerate(outs):
        start = pl.multiple_of((group ^ flip) * block, LANES)
        out[:, :width] = tok[...]
        out[:, width : width + block] = cot[:, pl.ds(start, block)]
        out[:, width + block :] = table


def pack_rows(tokens, cotangent, ids, gates, groups):
    rows, width = tokens.shape
    return pl.pallas_call(
        pack_rows_kernel,
        out_shape=[pltpu.VMEM((rows, width + width // groups + LANES), BF16)] * groups,
        in_specs=[whole()] * 4,
        name="pack_rows",
    )(tokens, cotangent, ids.T, gates.T)


def swap_halves(x):
    return jnp.concatenate([x[:, HALF:], x[:, :HALF]], axis=1)


def low_half(shape):
    return lax.broadcasted_iota(jnp.int32, shape, 1) < HALF


def pack_weights_kernel(weights, *outs):
    groups = len(outs)
    hidden_units = weights.shape[1] // 2
    group = lax.axis_index("dp")
    low = low_half((weights.shape[0], LANES))
    for pair in range(groups // 2):
        gate, up = (
            [
                weights[:, start + i * LANES : start + (i + 1) * LANES]
                for i in range(pair * 3, pair * 3 + 3)
            ]
            for start in (0, hidden_units)
        )
        even = gate[0], up[0], jnp.where(low, gate[1], swap_halves(up[1]))
        odd = (
            swap_halves(jnp.where(low, gate[2], gate[1])),
            swap_halves(jnp.where(low, up[2], up[1])),
            jnp.where(low, swap_halves(up[2]), gate[2]),
        )
        for parity, tiles in enumerate((even, odd)):
            for flip, out in enumerate(outs):

                @pl.when((group ^ flip) == 2 * pair + parity)
                def _():
                    for i, tile in enumerate(tiles):
                        out[:, i * LANES : (i + 1) * LANES] = tile


def pack_weights(weights, groups):
    rows, cols = weights.shape
    return pl.pallas_call(
        pack_weights_kernel,
        out_shape=[pltpu.VMEM((rows, cols // groups), BF16)] * groups,
        in_specs=[whole()],
        compiler_params=pltpu.CompilerParams(vmem_limit_bytes=VMEM_BYTES),
        name="pack_weights",
    )(weights)


def after(x, *others):
    return lax.optimization_barrier((x, *others))[0]


def in_vmem(x):
    return pltpu.with_memory_space_constraint(x, pltpu.VMEM)


def order_groups_kernel(*refs):
    *blocks, out = refs
    for flip, block in enumerate(blocks):
        out[pl.ds(lax.axis_index("dp") ^ flip, 1)] = block[...][None]


def order_groups(blocks):
    rows, width = blocks[0].shape
    out = pl.pallas_call(
        order_groups_kernel,
        out_shape=pltpu.VMEM((len(blocks), rows, width), BF16),
        in_specs=[whole()] * len(blocks),
        name="order_groups",
    )(*[in_vmem(x) for x in blocks])
    return out.reshape(len(blocks) * rows, width)


def silu(x):
    return x / (1.0 + jnp.exp(-x))


def start_kernel(pieces, flips, *refs):
    row_refs, refs = refs[:pieces], refs[pieces:]
    weight_refs, (pre, kept, toks) = refs[: len(flips)], refs[len(flips) :]
    rows, width = row_refs[0].shape
    block = weight_refs[0].shape[0]
    group = lax.axis_index("dp")
    for i, ref in enumerate(row_refs):
        toks[i * rows : (i + 1) * rows, :] = ref[...]
    total = None
    for flip, ref in zip(flips, weight_refs, strict=True):
        start = pl.multiple_of((group ^ flip) * block, LANES)
        term = jnp.dot(toks[:, pl.ds(start, block)], ref[...], preferred_element_type=F32)
        total = term if total is None else total + term
    pre[...] = total
    rest = sorted(set(range(lax.axis_size("dp"))) - set(flips))
    for i, flip in enumerate(rest):
        start = pl.multiple_of((group ^ flip) * block, LANES)
        kept[:, i * block : (i + 1) * block] = toks[:, pl.ds(start, block)]


def start_hidden(pieces, weights, flips, width):
    rows = pieces[0].shape[0]
    total = rows * len(pieces)
    block, cols = weights[0].shape
    left = width - block * len(flips)
    return pl.pallas_call(
        functools.partial(start_kernel, len(pieces), flips),
        out_shape=[pltpu.VMEM((total, cols), F32), pltpu.VMEM((total, left), BF16)],
        grid=(1,),
        in_specs=[pl.BlockSpec((rows, width), lambda i: (0, 0))] * len(pieces)
        + [pl.BlockSpec((block, cols), lambda i: (0, 0))] * len(weights),
        out_specs=[
            pl.BlockSpec((total, cols), lambda i: (0, 0)),
            pl.BlockSpec((total, left), lambda i: (0, 0)),
        ],
        scratch_shapes=[pltpu.VMEM((total, width), BF16)],
        compiler_params=pltpu.CompilerParams(vmem_limit_bytes=VMEM_BYTES),
        name="start_hidden",
    )(*[in_vmem(x) for x in [*pieces, *weights]])


def hidden_kernel(partial, rows, *refs):
    *weights, hidden = refs
    pre = partial[...]
    for i, ref in enumerate(weights):
        block = ref.shape[0]
        part = rows[:, i * block : (i + 1) * block]
        pre = pre + jnp.dot(part, ref[...], preferred_element_type=F32)
    gate, up, shared = (pre[:, i * LANES : (i + 1) * LANES] for i in range(3))
    hidden[:LANES, :] = (silu(gate) * up).T.astype(BF16)
    halves = (silu(shared) * swap_halves(shared)).T.astype(BF16)
    for parity in range(2):

        @pl.when(lax.rem(lax.axis_index("dp"), 2) == parity)
        def _():
            hidden[LANES:, :] = halves[parity * HALF : (parity + 1) * HALF]


def end_hidden(partial, rows, weights):
    args = [partial, rows, *weights]
    return pl.pallas_call(
        hidden_kernel,
        out_shape=pltpu.VMEM((partial.shape[1] // 2, rows.shape[0]), BF16),
        in_specs=[whole()] * len(args),
        compiler_params=pltpu.CompilerParams(vmem_limit_bytes=VMEM_BYTES),
        name="end_hidden",
    )(*[in_vmem(x) for x in args])


def scaled_kernel(start, *refs):
    *pieces, out = refs
    rows, block = pieces[0].shape[0], out.shape[1]
    blocks = []
    for piece in pieces:
        gates = piece[:, start + block :].astype(F32)
        lane = lax.broadcasted_iota(jnp.int32, gates.shape, 1)
        here = lane == lax.axis_index("expert")
        gate = jnp.sum(jnp.where(here, gates, 0.0), axis=1, keepdims=True)
        cot = piece[:, start : start + block].astype(F32)
        blocks.append((gate * cot).astype(BF16))
    out[...] = jnp.concatenate(blocks, axis=0)


def scaled_rows(pieces, width, block):
    total = pieces[0].shape[0] * len(pieces)
    return pl.pallas_call(
        functools.partial(scaled_kernel, width),
        out_shape=pltpu.VMEM((total, block), BF16),
        in_specs=[whole()] * len(pieces),
        compiler_params=pltpu.CompilerParams(vmem_limit_bytes=VMEM_BYTES),
        name="scaled_rows",
    )(*[in_vmem(x) for x in pieces])


def flip_kernel(*refs):
    half = len(refs) // 2
    for x, out in zip(refs[:half], refs[half:], strict=True):
        out[...] = x[...].T


def transposed(*arrays):
    return pl.pallas_call(
        flip_kernel,
        out_shape=[pltpu.VMEM(x.shape[::-1], x.dtype) for x in arrays],
        in_specs=[whole()] * len(arrays),
        compiler_params=pltpu.CompilerParams(vmem_limit_bytes=VMEM_BYTES),
        name="transposed",
    )(*arrays)


def update_kernel(flips, *refs):
    groups = lax.axis_size("dp")
    count = len(flips)
    hid_refs, (scaled, down, first, second), refs = refs[:count], refs[count : count + 4], refs[count + 4 :]
    outs, hidden = refs[:-1], refs[-1]
    cols = down.shape[0] // groups
    for i, ref in enumerate(hid_refs):
        hidden[i * cols : (i + 1) * cols, :] = ref[...]
    for chip_flip, out in enumerate(outs):
        tile = (lax.axis_index("expert") // CORES) ^ chip_flip
        lanes = pl.ds(pl.multiple_of(tile * LANES, LANES), LANES)
        grad = jnp.dot(hidden[...], scaled[:, lanes], preferred_element_type=F32)
        for i, flip in enumerate(flips):
            at = pl.multiple_of((lax.axis_index("dp") ^ flip) * cols, 16)
            here = pl.ds(at, cols), lanes
            part = grad[i * cols : (i + 1) * cols]
            out[i] = adam(down[here], first[here], second[here], part)


def update_tiles(hidden, flips, scaled, state, chips):
    cols, total = hidden[0].shape
    count = len(flips)
    return pl.pallas_call(
        functools.partial(update_kernel, flips),
        out_shape=[pltpu.VMEM((count, cols, scaled.shape[1] // chips), BF16)] * chips,
        in_specs=[whole()] * (count + 4),
        scratch_shapes=[pltpu.VMEM((count * cols, total), BF16)],
        compiler_params=pltpu.CompilerParams(vmem_limit_bytes=VMEM_BYTES),
        name="update_tiles",
    )(*[in_vmem(x) for x in [*hidden, scaled, *state]])


def regroup_kernel(*refs):
    chips = lax.axis_size("expert") // CORES
    tiles, outs = refs[:chips], refs[chips:]
    own = lax.axis_index("expert") // CORES
    for flip, tile in enumerate(tiles):
        for other, out in enumerate(outs):
            out[pl.ds(own ^ flip, 1)] = tile[other][None]


def regroup(tiles):
    groups, *tile = tiles[0].shape
    return pl.pallas_call(
        regroup_kernel,
        out_shape=[pltpu.VMEM((len(tiles), *tile), BF16)] * groups,
        in_specs=[whole()] * len(tiles),
        name="regroup",
    )(*[in_vmem(x) for x in tiles])


def pick_kernel(count, order, *refs):
    kept, swapped, outs = refs[:count], refs[count : 2 * count], refs[2 * count :]
    spot = lax.axis_index("expert")
    core = lax.rem(spot, CORES)
    for flip, out in enumerate(outs):
        source = order[spot ^ (flip * CORES)]
        chip, here = source // CORES, lax.rem(source, CORES) == core

        @pl.when(here)
        def _():
            for i in range(count):
                out[i] = kept[i][chip]

        @pl.when(jnp.logical_not(here))
        def _():
            for i in range(count):
                out[i] = swapped[i][chip]


def pick(order, kept, swapped):
    chips, *tile = kept[0].shape
    count = len(kept)
    return pl.pallas_call(
        functools.partial(pick_kernel, count),
        out_shape=[pltpu.VMEM((count, *tile), BF16)] * chips,
        in_specs=[smem()] + [whole()] * (2 * count),
        name="pick",
    )(order, *[in_vmem(x) for x in [*kept, *swapped]])


def unpack_kernel(sets, *refs):
    *pieces, out = refs
    chips = len(pieces) // len(sets)
    block = out.shape[2] // sum(map(len, sets))
    for i, piece in enumerate(pieces):
        tile = (lax.axis_index("expert") // CORES) ^ (i % chips)
        for j, flip in enumerate(sets[i // chips]):
            left = (lax.axis_index("dp") ^ flip) * block + tile * LANES
            out[0, :, pl.ds(pl.multiple_of(left, LANES), LANES)] = piece[j]


def unpack(pieces, sets, width, cols):
    return pl.pallas_call(
        functools.partial(unpack_kernel, sets),
        out_shape=jax.ShapeDtypeStruct((1, cols, width), BF16),
        in_specs=[whole()] * len(pieces),
        out_specs=whole(),
        name="unpack",
    )(*[in_vmem(x) for x in pieces])


def dense(tokens, cotangent, route_ids, route_gates, gate_up, down, moment1, moment2, placement):
    experts = lax.axis_size("expert")
    groups = lax.axis_size("dp")
    width = tokens.shape[1]
    units = down.shape[2]
    block = width // groups

    own, near, far, farthest = pack_weights(gate_up[0], groups)
    sent = pack_rows(tokens, cotangent, route_ids, route_gates, groups)
    blocks = [sent[0]] + [partner(sent[k], "dp", k) for k in range(1, groups)]
    state = transposed(down[0], moment1[0], moment2[0])
    plane = order_groups([after(blocks[0], state[0]), *blocks[1:]])
    chips = [plane] + [partner(plane, "expert", k) for k in range(2, experts, 2)]
    pieces = chips + [partner(x, "expert", 1) for x in chips]
    far = partner(after(far, blocks[1]), "dp", 2)
    near = partner(after(near, chips[1]), "dp", 1)
    farthest = partner(after(farthest, far), "dp", 3)

    cols = units // groups
    partial, rows = start_hidden(pieces, [own, far, near], (0, 2, 1), width)
    part = end_hidden(partial, rows, [farthest])
    scaled = scaled_rows(pieces, width, block)
    across = partner(part, "dp", 2)
    hidden = [part, partner(part, "dp", 1), across, partner(across, "dp", 1)]
    planes = experts // CORES
    sets = (0, 2), (1, 3)
    landed = []
    for flips in sets:
        tiles = update_tiles([hidden[k] for k in flips], flips, scaled, state, planes)
        tiles = [tiles[0]] + [
            partner(tiles[k], "expert", k * CORES) for k in range(1, planes)
        ]
        split = regroup(tiles)
        kept = [
            partner(x, "dp", k) if k else x for k, x in zip(flips, split, strict=True)
        ]
        swapped = [partner(x, "expert", 1) for x in kept]
        picked = pick(placement, kept, swapped)
        landed += [picked[0]] + [
            partner(picked[k], "expert", k * CORES) for k in range(1, planes)
        ]
    return unpack(landed, sets, width, cols).transpose(0, 2, 1)


def shards(tokens, cotangent, route_ids, *rest):
    every = route_ids.shape[1] == lax.axis_size("expert")
    return (dense if every else routed)(tokens, cotangent, route_ids, *rest)


def solution(mesh):
    placed = (
        P(("expert", "dp"), None),
        P(("expert", "dp"), None),
        P(("expert", "dp"), None),
        P(("expert", "dp"), None),
        P("expert", "dp", None),
        P("expert", "dp", None),
        P("expert", "dp", None),
        P("expert", "dp", None),
        P(),
    )
    return jax.shard_map(
        shards, mesh=mesh, in_specs=placed, out_specs=P("expert", None, "dp"), check_vma=False
    )
```

```python
import functools

import jax
import jax.numpy as jnp
from jax import lax
from jax.experimental import pallas as pl
from jax.experimental.pallas import tpu as pltpu
from jax.sharding import PartitionSpec as P

OPT_STEP = 2


BETA_ONE = 0.9
BETA_TWO = 0.95
ADAM_EPS = 1e-08
LEARN_RATE = 0.25

BF16 = jnp.bfloat16
F32 = jnp.float32
LANES = 128
HALF = LANES // 2
CORES = 2
VMEM_BYTES = 24 * 1024 * 1024


def adam(down, moment1, moment2, grad):
    correct_one = 1.0 - BETA_ONE**OPT_STEP
    correct_two = 1.0 - BETA_TWO**OPT_STEP
    first = BETA_ONE * moment1.astype(F32) + (1.0 - BETA_ONE) * grad
    second = BETA_TWO * moment2.astype(F32) + (1.0 - BETA_TWO) * grad * grad
    direction = first / correct_one / (jnp.sqrt(second / correct_two) + ADAM_EPS)
    return (down.astype(F32) - LEARN_RATE * direction).astype(BF16)


def routed(tokens, cotangent, route_ids, route_gates, gate_up, down, moment1, moment2, placement):
    experts = lax.axis_size("expert")
    tok_rows = tokens.shape[0]
    width = tokens.shape[1]
    top_count = route_ids.shape[1]
    hidden_units = down.shape[2]
    capacity = min(tok_rows, 2 * tok_rows * top_count // experts)
    total_slots = experts * capacity
    route_hits = jnp.sum(
        (route_ids[:, :, None] == jnp.arange(experts, dtype=jnp.int32)).astype(jnp.int32), axis=1
    )
    earlier_hits = jnp.cumsum(route_hits, axis=0) - route_hits
    slot_index = jnp.take_along_axis(earlier_hits, route_ids, axis=1)
    target_slot = route_ids * capacity + slot_index
    matched = (target_slot[:, :, None] == jnp.arange(total_slots, dtype=jnp.int32)).astype(F32)
    picker = jnp.sum(matched, axis=1).astype(BF16)
    contract_rows = (((0,), (0,)), ((), ()))
    send_rows = lax.dot_general(picker, tokens, contract_rows, preferred_element_type=F32)
    send_rows = send_rows.astype(BF16).reshape(experts, capacity, width)
    send_grads = lax.dot_general(picker, cotangent, contract_rows, preferred_element_type=F32)
    send_grads = send_grads.astype(BF16).reshape(experts, capacity, width)
    send_gates = jnp.sum(matched * route_gates.astype(F32)[:, :, None], axis=(0, 1))
    send_gates = send_gates.astype(BF16).reshape(experts, capacity)
    rows_in, grads_in, gates_in = (
        lax.all_to_all(send_rows, "expert", split_axis=0, concat_axis=0, tiled=True),
        lax.all_to_all(send_grads, "expert", split_axis=0, concat_axis=0, tiled=True),
        lax.all_to_all(send_gates, "expert", split_axis=0, concat_axis=0, tiled=True),
    )
    pre_all = jnp.dot(
        rows_in.reshape(total_slots, width),
        lax.all_gather(gate_up, "dp", axis=1, tiled=True)[0],
        preferred_element_type=F32,
    )
    hidden = (jax.nn.silu(pre_all[:, :hidden_units]) * pre_all[:, hidden_units:]).astype(BF16)
    scaled = gates_in.reshape(total_slots, 1).astype(F32) * grads_in.reshape(
        total_slots, width
    ).astype(F32)
    partial = lax.dot_general(
        scaled.astype(BF16), hidden, contract_rows, preferred_element_type=F32
    ).astype(BF16)
    grad_share = lax.psum_scatter(partial, "dp", scatter_dimension=0, tiled=True).astype(F32)
    updated = adam(down[0], moment1[0], moment2[0], grad_share)
    column_block = lax.all_to_all(updated, "dp", split_axis=1, concat_axis=0, tiled=True)
    block_cols = column_block.shape[1]
    piece_flat = column_block.reshape(experts, width * block_cols // experts)
    spread = lax.all_to_all(piece_flat, "expert", split_axis=0, concat_axis=0, tiled=True)
    picked = jnp.take(spread, placement, axis=0)
    landed = lax.all_to_all(picked, "expert", split_axis=0, concat_axis=0, tiled=True)
    return landed.reshape(1, width, block_cols)


def partner(x, axis, flip):
    size = lax.axis_size(axis)
    return lax.ppermute(x, axis, [(i, i ^ flip) for i in range(size)])


def smem():
    return pl.BlockSpec(memory_space=pltpu.SMEM)


def whole():
    return pl.BlockSpec(memory_space=pltpu.VMEM)


def pack_rows_kernel(tok, cot, ids, gates, *outs):
    groups = len(outs)
    width = tok.shape[1]
    block = width // groups
    group = lax.axis_index("dp")
    named = ids[...]
    weights = gates[...].astype(F32)
    expert = lax.broadcasted_iota(jnp.int32, (LANES, named.shape[1]), 0)
    table = jnp.zeros(expert.shape, F32)
    for k in range(named.shape[0]):
        table = table + jnp.where(expert == named[k : k + 1, :], weights[k : k + 1, :], 0.0)
    table = table.T.astype(BF16)
    for flip, out in enumerate(outs):
        start = pl.multiple_of((group ^ flip) * block, LANES)
        out[:, :width] = tok[...]
        out[:, width : width + block] = cot[:, pl.ds(start, block)]
        out[:, width + block :] = table


def pack_rows(tokens, cotangent, ids, gates, groups):
    rows, width = tokens.shape
    return pl.pallas_call(
        pack_rows_kernel,
        out_shape=[pltpu.VMEM((rows, width + width // groups + LANES), BF16)] * groups,
        in_specs=[whole()] * 4,
        name="pack_rows",
    )(tokens, cotangent, ids.T, gates.T)


def swap_halves(x):
    return jnp.concatenate([x[:, HALF:], x[:, :HALF]], axis=1)


def low_half(shape):
    return lax.broadcasted_iota(jnp.int32, shape, 1) < HALF


def pack_weights_kernel(weights, *outs):
    groups = len(outs)
    hidden_units = weights.shape[1] // 2
    group = lax.axis_index("dp")
    low = low_half((weights.shape[0], LANES))
    for pair in range(groups // 2):
        gate, up = (
            [
                weights[:, start + i * LANES : start + (i + 1) * LANES]
                for i in range(pair * 3, pair * 3 + 3)
            ]
            for start in (0, hidden_units)
        )
        even = gate[0], up[0], jnp.where(low, gate[1], swap_halves(up[1]))
        odd = (
            swap_halves(jnp.where(low, gate[2], gate[1])),
            swap_halves(jnp.where(low, up[2], up[1])),
            jnp.where(low, swap_halves(up[2]), gate[2]),
        )
        for parity, tiles in enumerate((even, odd)):
            for flip, out in enumerate(outs):

                @pl.when((group ^ flip) == 2 * pair + parity)
                def _():
                    for i, tile in enumerate(tiles):
                        out[:, i * LANES : (i + 1) * LANES] = tile


def pack_weights(weights, groups):
    rows, cols = weights.shape
    return pl.pallas_call(
        pack_weights_kernel,
        out_shape=[pltpu.VMEM((rows, cols // groups), BF16)] * groups,
        in_specs=[whole()],
        compiler_params=pltpu.CompilerParams(vmem_limit_bytes=VMEM_BYTES),
        name="pack_weights",
    )(weights)


def after(x, *others):
    return lax.optimization_barrier((x, *others))[0]


def in_vmem(x):
    return pltpu.with_memory_space_constraint(x, pltpu.VMEM)


def order_groups_kernel(*refs):
    *blocks, out = refs
    for flip, block in enumerate(blocks):
        out[pl.ds(lax.axis_index("dp") ^ flip, 1)] = block[...][None]


def order_groups(blocks):
    rows, width = blocks[0].shape
    out = pl.pallas_call(
        order_groups_kernel,
        out_shape=pltpu.VMEM((len(blocks), rows, width), BF16),
        in_specs=[whole()] * len(blocks),
        name="order_groups",
    )(*[in_vmem(x) for x in blocks])
    return out.reshape(len(blocks) * rows, width)


def silu(x):
    return x / (1.0 + jnp.exp(-x))


def start_kernel(pieces, flips, *refs):
    row_refs, refs = refs[:pieces], refs[pieces:]
    weight_refs, (pre, kept, toks) = refs[: len(flips)], refs[len(flips) :]
    rows, width = row_refs[0].shape
    block = weight_refs[0].shape[0]
    group = lax.axis_index("dp")
    for i, ref in enumerate(row_refs):
        toks[i * rows : (i + 1) * rows, :] = ref[...]
    total = None
    for flip, ref in zip(flips, weight_refs, strict=True):
        start = pl.multiple_of((group ^ flip) * block, LANES)
        term = jnp.dot(toks[:, pl.ds(start, block)], ref[...], preferred_element_type=F32)
        total = term if total is None else total + term
    pre[...] = total
    rest = sorted(set(range(lax.axis_size("dp"))) - set(flips))
    for i, flip in enumerate(rest):
        start = pl.multiple_of((group ^ flip) * block, LANES)
        kept[:, i * block : (i + 1) * block] = toks[:, pl.ds(start, block)]


def start_hidden(pieces, weights, flips, width):
    rows = pieces[0].shape[0]
    total = rows * len(pieces)
    block, cols = weights[0].shape
    left = width - block * len(flips)
    return pl.pallas_call(
        functools.partial(start_kernel, len(pieces), flips),
        out_shape=[pltpu.VMEM((total, cols), F32), pltpu.VMEM((total, left), BF16)],
        grid=(1,),
        in_specs=[pl.BlockSpec((rows, width), lambda i: (0, 0))] * len(pieces)
        + [pl.BlockSpec((block, cols), lambda i: (0, 0))] * len(weights),
        out_specs=[
            pl.BlockSpec((total, cols), lambda i: (0, 0)),
            pl.BlockSpec((total, left), lambda i: (0, 0)),
        ],
        scratch_shapes=[pltpu.VMEM((total, width), BF16)],
        compiler_params=pltpu.CompilerParams(vmem_limit_bytes=VMEM_BYTES),
        name="start_hidden",
    )(*[in_vmem(x) for x in [*pieces, *weights]])


def hidden_kernel(partial, rows, *refs):
    *weights, hidden = refs
    pre = partial[...]
    for i, ref in enumerate(weights):
        block = ref.shape[0]
        part = rows[:, i * block : (i + 1) * block]
        pre = pre + jnp.dot(part, ref[...], preferred_element_type=F32)
    gate, up, shared = (pre[:, i * LANES : (i + 1) * LANES] for i in range(3))
    hidden[:LANES, :] = (silu(gate) * up).T.astype(BF16)
    halves = (silu(shared) * swap_halves(shared)).T.astype(BF16)
    for parity in range(2):

        @pl.when(lax.rem(lax.axis_index("dp"), 2) == parity)
        def _():
            hidden[LANES:, :] = halves[parity * HALF : (parity + 1) * HALF]


def end_hidden(partial, rows, weights):
    args = [partial, rows, *weights]
    return pl.pallas_call(
        hidden_kernel,
        out_shape=pltpu.VMEM((partial.shape[1] // 2, rows.shape[0]), BF16),
        in_specs=[whole()] * len(args),
        compiler_params=pltpu.CompilerParams(vmem_limit_bytes=VMEM_BYTES),
        name="end_hidden",
    )(*[in_vmem(x) for x in args])


def scaled_kernel(start, *refs):
    *pieces, out = refs
    rows, block = pieces[0].shape[0], out.shape[1]
    blocks = []
    for piece in pieces:
        gates = piece[:, start + block :].astype(F32)
        lane = lax.broadcasted_iota(jnp.int32, gates.shape, 1)
        here = lane == lax.axis_index("expert")
        gate = jnp.sum(jnp.where(here, gates, 0.0), axis=1, keepdims=True)
        cot = piece[:, start : start + block].astype(F32)
        blocks.append((gate * cot).astype(BF16))
    out[...] = jnp.concatenate(blocks, axis=0)


def scaled_rows(pieces, width, block):
    total = pieces[0].shape[0] * len(pieces)
    return pl.pallas_call(
        functools.partial(scaled_kernel, width),
        out_shape=pltpu.VMEM((total, block), BF16),
        in_specs=[whole()] * len(pieces),
        compiler_params=pltpu.CompilerParams(vmem_limit_bytes=VMEM_BYTES),
        name="scaled_rows",
    )(*[in_vmem(x) for x in pieces])


def flip_kernel(*refs):
    half = len(refs) // 2
    for x, out in zip(refs[:half], refs[half:], strict=True):
        out[...] = x[...].T


def transposed(*arrays):
    return pl.pallas_call(
        flip_kernel,
        out_shape=[pltpu.VMEM(x.shape[::-1], x.dtype) for x in arrays],
        in_specs=[whole()] * len(arrays),
        compiler_params=pltpu.CompilerParams(vmem_limit_bytes=VMEM_BYTES),
        name="transposed",
    )(*arrays)


def update_kernel(flips, *refs):
    groups = lax.axis_size("dp")
    count = len(flips)
    hid_refs, (scaled, down, first, second), refs = refs[:count], refs[count : count + 4], refs[count + 4 :]
    outs, hidden = refs[:-1], refs[-1]
    cols = down.shape[0] // groups
    for i, ref in enumerate(hid_refs):
        hidden[i * cols : (i + 1) * cols, :] = ref[...]
    for chip_flip, out in enumerate(outs):
        tile = (lax.axis_index("expert") // CORES) ^ chip_flip
        lanes = pl.ds(pl.multiple_of(tile * LANES, LANES), LANES)
        grad = jnp.dot(hidden[...], scaled[:, lanes], preferred_element_type=F32)
        for i, flip in enumerate(flips):
            at = pl.multiple_of((lax.axis_index("dp") ^ flip) * cols, 16)
            here = pl.ds(at, cols), lanes
            part = grad[i * cols : (i + 1) * cols]
            out[i] = adam(down[here], first[here], second[here], part)


def update_tiles(hidden, flips, scaled, state, chips):
    cols, total = hidden[0].shape
    count = len(flips)
    return pl.pallas_call(
        functools.partial(update_kernel, flips),
        out_shape=[pltpu.VMEM((count, cols, scaled.shape[1] // chips), BF16)] * chips,
        in_specs=[whole()] * (count + 4),
        scratch_shapes=[pltpu.VMEM((count * cols, total), BF16)],
        compiler_params=pltpu.CompilerParams(vmem_limit_bytes=VMEM_BYTES),
        name="update_tiles",
    )(*[in_vmem(x) for x in [*hidden, scaled, *state]])


def regroup_kernel(*refs):
    chips = lax.axis_size("expert") // CORES
    tiles, outs = refs[:chips], refs[chips:]
    own = lax.axis_index("expert") // CORES
    for flip, tile in enumerate(tiles):
        for other, out in enumerate(outs):
            out[pl.ds(own ^ flip, 1)] = tile[other][None]


def regroup(tiles):
    groups, *tile = tiles[0].shape
    return pl.pallas_call(
        regroup_kernel,
        out_shape=[pltpu.VMEM((len(tiles), *tile), BF16)] * groups,
        in_specs=[whole()] * len(tiles),
        name="regroup",
    )(*[in_vmem(x) for x in tiles])


def pick_kernel(count, order, *refs):
    kept, swapped, outs = refs[:count], refs[count : 2 * count], refs[2 * count :]
    spot = lax.axis_index("expert")
    core = lax.rem(spot, CORES)
    for flip, out in enumerate(outs):
        source = order[spot ^ (flip * CORES)]
        chip, here = source // CORES, lax.rem(source, CORES) == core

        @pl.when(here)
        def _():
            for i in range(count):
                out[i] = kept[i][chip]

        @pl.when(jnp.logical_not(here))
        def _():
            for i in range(count):
                out[i] = swapped[i][chip]


def pick(order, kept, swapped):
    chips, *tile = kept[0].shape
    count = len(kept)
    return pl.pallas_call(
        functools.partial(pick_kernel, count),
        out_shape=[pltpu.VMEM((count, *tile), BF16)] * chips,
        in_specs=[smem()] + [whole()] * (2 * count),
        name="pick",
    )(order, *[in_vmem(x) for x in [*kept, *swapped]])


def unpack_kernel(sets, *refs):
    *pieces, out = refs
    chips = len(pieces) // len(sets)
    block = out.shape[2] // sum(map(len, sets))
    for i, piece in enumerate(pieces):
        tile = (lax.axis_index("expert") // CORES) ^ (i % chips)
        for j, flip in enumerate(sets[i // chips]):
            left = (lax.axis_index("dp") ^ flip) * block + tile * LANES
            out[0, :, pl.ds(pl.multiple_of(left, LANES), LANES)] = piece[j]


def unpack(pieces, sets, width, cols):
    return pl.pallas_call(
        functools.partial(unpack_kernel, sets),
        out_shape=jax.ShapeDtypeStruct((1, cols, width), BF16),
        in_specs=[whole()] * len(pieces),
        out_specs=whole(),
        name="unpack",
    )(*[in_vmem(x) for x in pieces])


def dense(tokens, cotangent, route_ids, route_gates, gate_up, down, moment1, moment2, placement):
    experts = lax.axis_size("expert")
    groups = lax.axis_size("dp")
    width = tokens.shape[1]
    units = down.shape[2]
    block = width // groups

    own, near, far, farthest = pack_weights(gate_up[0], groups)
    sent = pack_rows(tokens, cotangent, route_ids, route_gates, groups)
    blocks = [sent[0]] + [partner(sent[k], "dp", k) for k in range(1, groups)]
    state = transposed(down[0], moment1[0], moment2[0])
    plane = order_groups([after(blocks[0], state[0]), *blocks[1:]])
    chips = [plane] + [partner(plane, "expert", k) for k in range(2, experts, 2)]
    pieces = chips + [partner(x, "expert", 1) for x in chips]
    far = partner(after(far, blocks[1]), "dp", 2)
    near = partner(after(near, chips[1]), "dp", 1)
    farthest = partner(after(farthest, far), "dp", 3)

    cols = units // groups
    partial, rows = start_hidden(pieces, [own, far, near], (0, 2, 1), width)
    part = end_hidden(partial, rows, [farthest])
    scaled = scaled_rows(pieces, width, block)
    across = partner(part, "dp", 2)
    hidden = [part, partner(part, "dp", 1), across, partner(across, "dp", 1)]
    planes = experts // CORES
    kept = {}
    for flips in ((0, 3), (1, 2)):
        tiles = update_tiles([hidden[k] for k in flips], flips, scaled, state, planes)
        tiles = [tiles[0]] + [
            partner(tiles[k], "expert", k * CORES) for k in range(1, planes)
        ]
        for k, x in zip(flips, regroup(tiles), strict=True):
            kept[k] = partner(x, "dp", k) if k else x
    swapped = {k: partner(x, "expert", 1) for k, x in kept.items()}
    sets = ((1, 0), (3, 2))
    landed = []
    for flips in sets:
        picked = pick(placement, [kept[k] for k in flips], [swapped[k] for k in flips])
        landed += [picked[0]] + [
            partner(picked[k], "expert", k * CORES) for k in range(1, planes)
        ]
    return unpack(landed, sets, width, cols).transpose(0, 2, 1)


def shards(tokens, cotangent, route_ids, *rest):
    every = route_ids.shape[1] == lax.axis_size("expert")
    return (dense if every else routed)(tokens, cotangent, route_ids, *rest)


def solution(mesh):
    placed = (
        P(("expert", "dp"), None),
        P(("expert", "dp"), None),
        P(("expert", "dp"), None),
        P(("expert", "dp"), None),
        P("expert", "dp", None),
        P("expert", "dp", None),
        P("expert", "dp", None),
        P("expert", "dp", None),
        P(),
    )
    return jax.shard_map(
        shards, mesh=mesh, in_specs=placed, out_specs=P("expert", None, "dp"), check_vma=False
    )
```

```python
import functools

import jax
import jax.numpy as jnp
from jax import lax
from jax.experimental import pallas as pl
from jax.experimental.pallas import tpu as pltpu
from jax.sharding import PartitionSpec as P

OPT_STEP = 2


BETA_ONE = 0.9
BETA_TWO = 0.95
ADAM_EPS = 1e-08
LEARN_RATE = 0.25

BF16 = jnp.bfloat16
F32 = jnp.float32
LANES = 128
HALF = LANES // 2
CORES = 2
VMEM_BYTES = 24 * 1024 * 1024


def adam(down, moment1, moment2, grad):
    correct_one = 1.0 - BETA_ONE**OPT_STEP
    correct_two = 1.0 - BETA_TWO**OPT_STEP
    first = BETA_ONE * moment1.astype(F32) + (1.0 - BETA_ONE) * grad
    second = BETA_TWO * moment2.astype(F32) + (1.0 - BETA_TWO) * grad * grad
    direction = first / correct_one / (jnp.sqrt(second / correct_two) + ADAM_EPS)
    return (down.astype(F32) - LEARN_RATE * direction).astype(BF16)


def routed(tokens, cotangent, route_ids, route_gates, gate_up, down, moment1, moment2, placement):
    experts = lax.axis_size("expert")
    tok_rows = tokens.shape[0]
    width = tokens.shape[1]
    top_count = route_ids.shape[1]
    hidden_units = down.shape[2]
    capacity = min(tok_rows, 2 * tok_rows * top_count // experts)
    total_slots = experts * capacity
    route_hits = jnp.sum(
        (route_ids[:, :, None] == jnp.arange(experts, dtype=jnp.int32)).astype(jnp.int32), axis=1
    )
    earlier_hits = jnp.cumsum(route_hits, axis=0) - route_hits
    slot_index = jnp.take_along_axis(earlier_hits, route_ids, axis=1)
    target_slot = route_ids * capacity + slot_index
    matched = (target_slot[:, :, None] == jnp.arange(total_slots, dtype=jnp.int32)).astype(F32)
    picker = jnp.sum(matched, axis=1).astype(BF16)
    contract_rows = (((0,), (0,)), ((), ()))
    send_rows = lax.dot_general(picker, tokens, contract_rows, preferred_element_type=F32)
    send_rows = send_rows.astype(BF16).reshape(experts, capacity, width)
    send_grads = lax.dot_general(picker, cotangent, contract_rows, preferred_element_type=F32)
    send_grads = send_grads.astype(BF16).reshape(experts, capacity, width)
    send_gates = jnp.sum(matched * route_gates.astype(F32)[:, :, None], axis=(0, 1))
    send_gates = send_gates.astype(BF16).reshape(experts, capacity)
    rows_in, grads_in, gates_in = (
        lax.all_to_all(send_rows, "expert", split_axis=0, concat_axis=0, tiled=True),
        lax.all_to_all(send_grads, "expert", split_axis=0, concat_axis=0, tiled=True),
        lax.all_to_all(send_gates, "expert", split_axis=0, concat_axis=0, tiled=True),
    )
    pre_all = jnp.dot(
        rows_in.reshape(total_slots, width),
        lax.all_gather(gate_up, "dp", axis=1, tiled=True)[0],
        preferred_element_type=F32,
    )
    hidden = (jax.nn.silu(pre_all[:, :hidden_units]) * pre_all[:, hidden_units:]).astype(BF16)
    scaled = gates_in.reshape(total_slots, 1).astype(F32) * grads_in.reshape(
        total_slots, width
    ).astype(F32)
    partial = lax.dot_general(
        scaled.astype(BF16), hidden, contract_rows, preferred_element_type=F32
    ).astype(BF16)
    grad_share = lax.psum_scatter(partial, "dp", scatter_dimension=0, tiled=True).astype(F32)
    updated = adam(down[0], moment1[0], moment2[0], grad_share)
    column_block = lax.all_to_all(updated, "dp", split_axis=1, concat_axis=0, tiled=True)
    block_cols = column_block.shape[1]
    piece_flat = column_block.reshape(experts, width * block_cols // experts)
    spread = lax.all_to_all(piece_flat, "expert", split_axis=0, concat_axis=0, tiled=True)
    picked = jnp.take(spread, placement, axis=0)
    landed = lax.all_to_all(picked, "expert", split_axis=0, concat_axis=0, tiled=True)
    return landed.reshape(1, width, block_cols)


def partner(x, axis, flip):
    size = lax.axis_size(axis)
    return lax.ppermute(x, axis, [(i, i ^ flip) for i in range(size)])


def smem():
    return pl.BlockSpec(memory_space=pltpu.SMEM)


def whole():
    return pl.BlockSpec(memory_space=pltpu.VMEM)


def pack_rows_kernel(tok, cot, ids, gates, *outs):
    groups = len(outs)
    width = tok.shape[1]
    block = width // groups
    group = lax.axis_index("dp")
    named = ids[...]
    weights = gates[...].astype(F32)
    expert = lax.broadcasted_iota(jnp.int32, (LANES, named.shape[1]), 0)
    table = jnp.zeros(expert.shape, F32)
    for k in range(named.shape[0]):
        table = table + jnp.where(expert == named[k : k + 1, :], weights[k : k + 1, :], 0.0)
    table = table.T.astype(BF16)
    for flip, out in enumerate(outs):
        start = pl.multiple_of((group ^ flip) * block, LANES)
        out[:, :width] = tok[...]
        out[:, width : width + block] = cot[:, pl.ds(start, block)]
        out[:, width + block :] = table


def pack_rows(tokens, cotangent, ids, gates, groups):
    rows, width = tokens.shape
    return pl.pallas_call(
        pack_rows_kernel,
        out_shape=[pltpu.VMEM((rows, width + width // groups + LANES), BF16)] * groups,
        in_specs=[whole()] * 4,
        name="pack_rows",
    )(tokens, cotangent, ids.T, gates.T)


def swap_halves(x):
    return jnp.concatenate([x[:, HALF:], x[:, :HALF]], axis=1)


def low_half(shape):
    return lax.broadcasted_iota(jnp.int32, shape, 1) < HALF


def pack_weights_kernel(weights, *outs):
    groups = len(outs)
    hidden_units = weights.shape[1] // 2
    group = lax.axis_index("dp")
    low = low_half((weights.shape[0], LANES))
    for pair in range(groups // 2):
        gate, up = (
            [
                weights[:, start + i * LANES : start + (i + 1) * LANES]
                for i in range(pair * 3, pair * 3 + 3)
            ]
            for start in (0, hidden_units)
        )
        even = gate[0], up[0], jnp.where(low, gate[1], swap_halves(up[1]))
        odd = (
            swap_halves(jnp.where(low, gate[2], gate[1])),
            swap_halves(jnp.where(low, up[2], up[1])),
            jnp.where(low, swap_halves(up[2]), gate[2]),
        )
        for parity, tiles in enumerate((even, odd)):
            for flip, out in enumerate(outs):

                @pl.when((group ^ flip) == 2 * pair + parity)
                def _():
                    for i, tile in enumerate(tiles):
                        out[:, i * LANES : (i + 1) * LANES] = tile


def pack_weights(weights, groups):
    rows, cols = weights.shape
    return pl.pallas_call(
        pack_weights_kernel,
        out_shape=[pltpu.VMEM((rows, cols // groups), BF16)] * groups,
        in_specs=[whole()],
        compiler_params=pltpu.CompilerParams(vmem_limit_bytes=VMEM_BYTES),
        name="pack_weights",
    )(weights)


def after(x, *others):
    return lax.optimization_barrier((x, *others))[0]


def in_vmem(x):
    return pltpu.with_memory_space_constraint(x, pltpu.VMEM)


def order_groups_kernel(*refs):
    *blocks, out = refs
    for flip, block in enumerate(blocks):
        out[pl.ds(lax.axis_index("dp") ^ flip, 1)] = block[...][None]


def order_groups(blocks):
    rows, width = blocks[0].shape
    out = pl.pallas_call(
        order_groups_kernel,
        out_shape=pltpu.VMEM((len(blocks), rows, width), BF16),
        in_specs=[whole()] * len(blocks),
        name="order_groups",
    )(*[in_vmem(x) for x in blocks])
    return out.reshape(len(blocks) * rows, width)


def silu(x):
    return x / (1.0 + jnp.exp(-x))


def start_kernel(pieces, flips, *refs):
    row_refs, refs = refs[:pieces], refs[pieces:]
    weight_refs, (pre, kept, toks) = refs[: len(flips)], refs[len(flips) :]
    rows, width = row_refs[0].shape
    block = weight_refs[0].shape[0]
    group = lax.axis_index("dp")
    for i, ref in enumerate(row_refs):
        toks[i * rows : (i + 1) * rows, :] = ref[...]
    total = None
    for flip, ref in zip(flips, weight_refs, strict=True):
        start = pl.multiple_of((group ^ flip) * block, LANES)
        term = jnp.dot(toks[:, pl.ds(start, block)], ref[...], preferred_element_type=F32)
        total = term if total is None else total + term
    pre[...] = total
    rest = sorted(set(range(lax.axis_size("dp"))) - set(flips))
    for i, flip in enumerate(rest):
        start = pl.multiple_of((group ^ flip) * block, LANES)
        kept[:, i * block : (i + 1) * block] = toks[:, pl.ds(start, block)]


def start_hidden(pieces, weights, flips, width):
    rows = pieces[0].shape[0]
    total = rows * len(pieces)
    block, cols = weights[0].shape
    left = width - block * len(flips)
    return pl.pallas_call(
        functools.partial(start_kernel, len(pieces), flips),
        out_shape=[pltpu.VMEM((total, cols), F32), pltpu.VMEM((total, left), BF16)],
        grid=(1,),
        in_specs=[pl.BlockSpec((rows, width), lambda i: (0, 0))] * len(pieces)
        + [pl.BlockSpec((block, cols), lambda i: (0, 0))] * len(weights),
        out_specs=[
            pl.BlockSpec((total, cols), lambda i: (0, 0)),
            pl.BlockSpec((total, left), lambda i: (0, 0)),
        ],
        scratch_shapes=[pltpu.VMEM((total, width), BF16)],
        compiler_params=pltpu.CompilerParams(vmem_limit_bytes=VMEM_BYTES),
        name="start_hidden",
    )(*[in_vmem(x) for x in [*pieces, *weights]])


def hidden_kernel(partial, rows, *refs):
    *weights, hidden = refs
    pre = partial[...]
    for i, ref in enumerate(weights):
        block = ref.shape[0]
        part = rows[:, i * block : (i + 1) * block]
        pre = pre + jnp.dot(part, ref[...], preferred_element_type=F32)
    gate, up, shared = (pre[:, i * LANES : (i + 1) * LANES] for i in range(3))
    hidden[:LANES, :] = (silu(gate) * up).T.astype(BF16)
    halves = (silu(shared) * swap_halves(shared)).T.astype(BF16)
    for parity in range(2):

        @pl.when(lax.rem(lax.axis_index("dp"), 2) == parity)
        def _():
            hidden[LANES:, :] = halves[parity * HALF : (parity + 1) * HALF]


def end_hidden(partial, rows, weights):
    args = [partial, rows, *weights]
    return pl.pallas_call(
        hidden_kernel,
        out_shape=pltpu.VMEM((partial.shape[1] // 2, rows.shape[0]), BF16),
        in_specs=[whole()] * len(args),
        compiler_params=pltpu.CompilerParams(vmem_limit_bytes=VMEM_BYTES),
        name="end_hidden",
    )(*[in_vmem(x) for x in args])


def scaled_kernel(start, *refs):
    *pieces, out = refs
    rows, block = pieces[0].shape[0], out.shape[1]
    blocks = []
    for piece in pieces:
        gates = piece[:, start + block :].astype(F32)
        lane = lax.broadcasted_iota(jnp.int32, gates.shape, 1)
        here = lane == lax.axis_index("expert")
        gate = jnp.sum(jnp.where(here, gates, 0.0), axis=1, keepdims=True)
        cot = piece[:, start : start + block].astype(F32)
        blocks.append((gate * cot).astype(BF16))
    out[...] = jnp.concatenate(blocks, axis=0)


def scaled_rows(pieces, width, block):
    total = pieces[0].shape[0] * len(pieces)
    return pl.pallas_call(
        functools.partial(scaled_kernel, width),
        out_shape=pltpu.VMEM((total, block), BF16),
        in_specs=[whole()] * len(pieces),
        compiler_params=pltpu.CompilerParams(vmem_limit_bytes=VMEM_BYTES),
        name="scaled_rows",
    )(*[in_vmem(x) for x in pieces])


def flip_kernel(*refs):
    half = len(refs) // 2
    for x, out in zip(refs[:half], refs[half:], strict=True):
        out[...] = x[...].T


def transposed(*arrays):
    return pl.pallas_call(
        flip_kernel,
        out_shape=[pltpu.VMEM(x.shape[::-1], x.dtype) for x in arrays],
        in_specs=[whole()] * len(arrays),
        compiler_params=pltpu.CompilerParams(vmem_limit_bytes=VMEM_BYTES),
        name="transposed",
    )(*arrays)


def update_kernel(flips, *refs):
    groups = lax.axis_size("dp")
    count = len(flips)
    hid_refs, (scaled, down, first, second), refs = refs[:count], refs[count : count + 4], refs[count + 4 :]
    outs, hidden = refs[:-1], refs[-1]
    cols = down.shape[0] // groups
    for i, ref in enumerate(hid_refs):
        hidden[i * cols : (i + 1) * cols, :] = ref[...]
    for chip_flip, out in enumerate(outs):
        tile = (lax.axis_index("expert") // CORES) ^ chip_flip
        lanes = pl.ds(pl.multiple_of(tile * LANES, LANES), LANES)
        grad = jnp.dot(hidden[...], scaled[:, lanes], preferred_element_type=F32)
        for i, flip in enumerate(flips):
            at = pl.multiple_of((lax.axis_index("dp") ^ flip) * cols, 16)
            here = pl.ds(at, cols), lanes
            part = grad[i * cols : (i + 1) * cols]
            out[i] = adam(down[here], first[here], second[here], part)


def update_tiles(hidden, flips, scaled, state, chips):
    cols, total = hidden[0].shape
    count = len(flips)
    return pl.pallas_call(
        functools.partial(update_kernel, flips),
        out_shape=[pltpu.VMEM((count, cols, scaled.shape[1] // chips), BF16)] * chips,
        in_specs=[whole()] * (count + 4),
        scratch_shapes=[pltpu.VMEM((count * cols, total), BF16)],
        compiler_params=pltpu.CompilerParams(vmem_limit_bytes=VMEM_BYTES),
        name="update_tiles",
    )(*[in_vmem(x) for x in [*hidden, scaled, *state]])


def regroup_kernel(*refs):
    chips = lax.axis_size("expert") // CORES
    tiles, outs = refs[:chips], refs[chips:]
    own = lax.axis_index("expert") // CORES
    for flip, tile in enumerate(tiles):
        for other, out in enumerate(outs):
            out[pl.ds(own ^ flip, 1)] = tile[other][None]


def regroup(tiles):
    groups, *tile = tiles[0].shape
    return pl.pallas_call(
        regroup_kernel,
        out_shape=[pltpu.VMEM((len(tiles), *tile), BF16)] * groups,
        in_specs=[whole()] * len(tiles),
        name="regroup",
    )(*[in_vmem(x) for x in tiles])


def pick_kernel(count, order, *refs):
    kept, swapped, outs = refs[:count], refs[count : 2 * count], refs[2 * count :]
    spot = lax.axis_index("expert")
    core = lax.rem(spot, CORES)
    for flip, out in enumerate(outs):
        source = order[spot ^ (flip * CORES)]
        chip, here = source // CORES, lax.rem(source, CORES) == core

        @pl.when(here)
        def _():
            for i in range(count):
                out[i] = kept[i][chip]

        @pl.when(jnp.logical_not(here))
        def _():
            for i in range(count):
                out[i] = swapped[i][chip]


def pick(order, kept, swapped):
    chips, *tile = kept[0].shape
    count = len(kept)
    return pl.pallas_call(
        functools.partial(pick_kernel, count),
        out_shape=[pltpu.VMEM((count, *tile), BF16)] * chips,
        in_specs=[smem()] + [whole()] * (2 * count),
        name="pick",
    )(order, *[in_vmem(x) for x in [*kept, *swapped]])


def unpack_kernel(flips, *refs):
    chips = lax.axis_size("expert") // CORES
    pieces, (out, sems) = refs[:chips], refs[-2:]
    block = out.shape[2] // lax.axis_size("dp")
    copies = []
    for i, piece in enumerate(pieces):
        tile = (lax.axis_index("expert") // CORES) ^ i
        for j, flip in enumerate(flips):
            left = (lax.axis_index("dp") ^ flip) * block + tile * LANES
            lanes = pl.ds(pl.multiple_of(left, LANES), LANES)
            copies.append(
                pltpu.make_async_copy(piece.at[j], out.at[0, :, lanes], sems.at[len(copies)])
            )
    for copy in copies:
        copy.start()
    for copy in copies:
        copy.wait()


def unpack(pieces, flips, width, cols, out):
    given = [] if out is None else [out]
    anywhere = pl.BlockSpec(memory_space=pl.ANY)
    return pl.pallas_call(
        functools.partial(unpack_kernel, flips),
        out_shape=jax.ShapeDtypeStruct((1, cols, width), BF16),
        in_specs=[whole()] * len(pieces) + [anywhere] * len(given),
        out_specs=anywhere,
        scratch_shapes=[pltpu.SemaphoreType.DMA((len(pieces) * len(flips),))],
        input_output_aliases={len(pieces): 0} if given else {},
        name="unpack",
    )(*[in_vmem(x) for x in pieces], *given)


def dense(tokens, cotangent, route_ids, route_gates, gate_up, down, moment1, moment2, placement):
    experts = lax.axis_size("expert")
    groups = lax.axis_size("dp")
    width = tokens.shape[1]
    units = down.shape[2]
    block = width // groups

    own, near, far, farthest = pack_weights(gate_up[0], groups)
    sent = pack_rows(tokens, cotangent, route_ids, route_gates, groups)
    blocks = [sent[0]] + [partner(sent[k], "dp", k) for k in range(1, groups)]
    state = transposed(down[0], moment1[0], moment2[0])
    plane = order_groups([after(blocks[0], state[0]), *blocks[1:]])
    chips = [plane] + [partner(plane, "expert", k) for k in range(2, experts, 2)]
    pieces = chips + [partner(x, "expert", 1) for x in chips]
    far = partner(after(far, blocks[1]), "dp", 2)
    near = partner(after(near, chips[1]), "dp", 1)
    farthest = partner(after(farthest, far), "dp", 3)

    cols = units // groups
    partial, rows = start_hidden(pieces, [own, far, near], (0, 2, 1), width)
    part = end_hidden(partial, rows, [farthest])
    scaled = scaled_rows(pieces, width, block)
    across = partner(part, "dp", 2)
    hidden = [part, partner(part, "dp", 1), across, partner(across, "dp", 1)]
    planes = experts // CORES
    kept = {}
    for flips in ((0, 3), (1, 2)):
        tiles = update_tiles([hidden[k] for k in flips], flips, scaled, state, planes)
        tiles = [tiles[0]] + [
            partner(tiles[k], "expert", k * CORES) for k in range(1, planes)
        ]
        for k, x in zip(flips, regroup(tiles), strict=True):
            kept[k] = partner(x, "dp", k) if k else x
    swapped = {k: partner(x, "expert", 1) for k, x in kept.items()}
    sets = ((1, 0), (3, 2))
    out = None
    for flips in sets:
        picked = pick(placement, [kept[k] for k in flips], [swapped[k] for k in flips])
        landed = [picked[0]] + [
            partner(picked[k], "expert", k * CORES) for k in range(1, planes)
        ]
        out = unpack(landed, flips, width, cols, out)
    return out.transpose(0, 2, 1)


def shards(tokens, cotangent, route_ids, *rest):
    every = route_ids.shape[1] == lax.axis_size("expert")
    return (dense if every else routed)(tokens, cotangent, route_ids, *rest)


def solution(mesh):
    placed = (
        P(("expert", "dp"), None),
        P(("expert", "dp"), None),
        P(("expert", "dp"), None),
        P(("expert", "dp"), None),
        P("expert", "dp", None),
        P("expert", "dp", None),
        P("expert", "dp", None),
        P("expert", "dp", None),
        P(),
    )
    return jax.shard_map(
        shards, mesh=mesh, in_specs=placed, out_specs=P("expert", None, "dp"), check_vma=False
    )
```

```python
import functools

import jax
import jax.numpy as jnp
from jax import lax
from jax.experimental import pallas as pl
from jax.experimental.pallas import tpu as pltpu
from jax.sharding import PartitionSpec as P

OPT_STEP = 2


BETA_ONE = 0.9
BETA_TWO = 0.95
ADAM_EPS = 1e-08
LEARN_RATE = 0.25

BF16 = jnp.bfloat16
F32 = jnp.float32
LANES = 128
HALF = LANES // 2
CORES = 2
VMEM_BYTES = 24 * 1024 * 1024


def adam(down, moment1, moment2, grad):
    correct_one = 1.0 - BETA_ONE**OPT_STEP
    correct_two = 1.0 - BETA_TWO**OPT_STEP
    first = BETA_ONE * moment1.astype(F32) + (1.0 - BETA_ONE) * grad
    second = BETA_TWO * moment2.astype(F32) + (1.0 - BETA_TWO) * grad * grad
    direction = first / correct_one / (jnp.sqrt(second / correct_two) + ADAM_EPS)
    return (down.astype(F32) - LEARN_RATE * direction).astype(BF16)


def routed(tokens, cotangent, route_ids, route_gates, gate_up, down, moment1, moment2, placement):
    experts = lax.axis_size("expert")
    tok_rows = tokens.shape[0]
    width = tokens.shape[1]
    top_count = route_ids.shape[1]
    hidden_units = down.shape[2]
    capacity = min(tok_rows, 2 * tok_rows * top_count // experts)
    total_slots = experts * capacity
    route_hits = jnp.sum(
        (route_ids[:, :, None] == jnp.arange(experts, dtype=jnp.int32)).astype(jnp.int32), axis=1
    )
    earlier_hits = jnp.cumsum(route_hits, axis=0) - route_hits
    slot_index = jnp.take_along_axis(earlier_hits, route_ids, axis=1)
    target_slot = route_ids * capacity + slot_index
    matched = (target_slot[:, :, None] == jnp.arange(total_slots, dtype=jnp.int32)).astype(F32)
    picker = jnp.sum(matched, axis=1).astype(BF16)
    contract_rows = (((0,), (0,)), ((), ()))
    send_rows = lax.dot_general(picker, tokens, contract_rows, preferred_element_type=F32)
    send_rows = send_rows.astype(BF16).reshape(experts, capacity, width)
    send_grads = lax.dot_general(picker, cotangent, contract_rows, preferred_element_type=F32)
    send_grads = send_grads.astype(BF16).reshape(experts, capacity, width)
    send_gates = jnp.sum(matched * route_gates.astype(F32)[:, :, None], axis=(0, 1))
    send_gates = send_gates.astype(BF16).reshape(experts, capacity)
    rows_in, grads_in, gates_in = (
        lax.all_to_all(send_rows, "expert", split_axis=0, concat_axis=0, tiled=True),
        lax.all_to_all(send_grads, "expert", split_axis=0, concat_axis=0, tiled=True),
        lax.all_to_all(send_gates, "expert", split_axis=0, concat_axis=0, tiled=True),
    )
    pre_all = jnp.dot(
        rows_in.reshape(total_slots, width),
        lax.all_gather(gate_up, "dp", axis=1, tiled=True)[0],
        preferred_element_type=F32,
    )
    hidden = (jax.nn.silu(pre_all[:, :hidden_units]) * pre_all[:, hidden_units:]).astype(BF16)
    scaled = gates_in.reshape(total_slots, 1).astype(F32) * grads_in.reshape(
        total_slots, width
    ).astype(F32)
    partial = lax.dot_general(
        scaled.astype(BF16), hidden, contract_rows, preferred_element_type=F32
    ).astype(BF16)
    grad_share = lax.psum_scatter(partial, "dp", scatter_dimension=0, tiled=True).astype(F32)
    updated = adam(down[0], moment1[0], moment2[0], grad_share)
    column_block = lax.all_to_all(updated, "dp", split_axis=1, concat_axis=0, tiled=True)
    block_cols = column_block.shape[1]
    piece_flat = column_block.reshape(experts, width * block_cols // experts)
    spread = lax.all_to_all(piece_flat, "expert", split_axis=0, concat_axis=0, tiled=True)
    picked = jnp.take(spread, placement, axis=0)
    landed = lax.all_to_all(picked, "expert", split_axis=0, concat_axis=0, tiled=True)
    return landed.reshape(1, width, block_cols)


def partner(x, axis, flip):
    size = lax.axis_size(axis)
    return lax.ppermute(x, axis, [(i, i ^ flip) for i in range(size)])


def smem():
    return pl.BlockSpec(memory_space=pltpu.SMEM)


def whole():
    return pl.BlockSpec(memory_space=pltpu.VMEM)


def pack_rows_kernel(tok, cot, ids, gates, *outs):
    groups = len(outs)
    width = tok.shape[1]
    block = width // groups
    group = lax.axis_index("dp")
    named = ids[...]
    weights = gates[...].astype(F32)
    expert = lax.broadcasted_iota(jnp.int32, (LANES, named.shape[1]), 0)
    table = jnp.zeros(expert.shape, F32)
    for k in range(named.shape[0]):
        table = table + jnp.where(expert == named[k : k + 1, :], weights[k : k + 1, :], 0.0)
    table = table.T.astype(BF16)
    for flip, out in enumerate(outs):
        start = pl.multiple_of((group ^ flip) * block, LANES)
        out[:, :width] = tok[...]
        out[:, width : width + block] = cot[:, pl.ds(start, block)]
        out[:, width + block :] = table


def pack_rows(tokens, cotangent, ids, gates, groups):
    rows, width = tokens.shape
    return pl.pallas_call(
        pack_rows_kernel,
        out_shape=[pltpu.VMEM((rows, width + width // groups + LANES), BF16)] * groups,
        in_specs=[whole()] * 4,
        name="pack_rows",
    )(tokens, cotangent, ids.T, gates.T)


def swap_halves(x):
    return jnp.concatenate([x[:, HALF:], x[:, :HALF]], axis=1)


def low_half(shape):
    return lax.broadcasted_iota(jnp.int32, shape, 1) < HALF


def pack_weights_kernel(weights, *outs):
    groups = len(outs)
    hidden_units = weights.shape[1] // 2
    group = lax.axis_index("dp")
    low = low_half((weights.shape[0], LANES))
    for pair in range(groups // 2):
        gate, up = (
            [
                weights[:, start + i * LANES : start + (i + 1) * LANES]
                for i in range(pair * 3, pair * 3 + 3)
            ]
            for start in (0, hidden_units)
        )
        even = gate[0], up[0], jnp.where(low, gate[1], swap_halves(up[1]))
        odd = (
            swap_halves(jnp.where(low, gate[2], gate[1])),
            swap_halves(jnp.where(low, up[2], up[1])),
            jnp.where(low, swap_halves(up[2]), gate[2]),
        )
        for parity, tiles in enumerate((even, odd)):
            for flip, out in enumerate(outs):

                @pl.when((group ^ flip) == 2 * pair + parity)
                def _():
                    for i, tile in enumerate(tiles):
                        out[:, i * LANES : (i + 1) * LANES] = tile


def pack_weights(weights, groups):
    rows, cols = weights.shape
    return pl.pallas_call(
        pack_weights_kernel,
        out_shape=[pltpu.VMEM((rows, cols // groups), BF16)] * groups,
        in_specs=[whole()],
        compiler_params=pltpu.CompilerParams(vmem_limit_bytes=VMEM_BYTES),
        name="pack_weights",
    )(weights)


def after(x, *others):
    return lax.optimization_barrier((x, *others))[0]


def in_vmem(x):
    return pltpu.with_memory_space_constraint(x, pltpu.VMEM)


def order_groups_kernel(*refs):
    *blocks, out = refs
    for flip, block in enumerate(blocks):
        out[pl.ds(lax.axis_index("dp") ^ flip, 1)] = block[...][None]


def order_groups(blocks):
    rows, width = blocks[0].shape
    out = pl.pallas_call(
        order_groups_kernel,
        out_shape=pltpu.VMEM((len(blocks), rows, width), BF16),
        in_specs=[whole()] * len(blocks),
        name="order_groups",
    )(*[in_vmem(x) for x in blocks])
    return out.reshape(len(blocks) * rows, width)


def silu(x):
    return x / (1.0 + jnp.exp(-x))


def start_kernel(pieces, flips, *refs):
    row_refs, refs = refs[:pieces], refs[pieces:]
    weight_refs, (pre, kept, toks) = refs[: len(flips)], refs[len(flips) :]
    rows, width = row_refs[0].shape
    block = weight_refs[0].shape[0]
    group = lax.axis_index("dp")
    for i, ref in enumerate(row_refs):
        toks[i * rows : (i + 1) * rows, :] = ref[...]
    total = None
    for flip, ref in zip(flips, weight_refs, strict=True):
        start = pl.multiple_of((group ^ flip) * block, LANES)
        term = jnp.dot(toks[:, pl.ds(start, block)], ref[...], preferred_element_type=F32)
        total = term if total is None else total + term
    pre[...] = total
    rest = sorted(set(range(lax.axis_size("dp"))) - set(flips))
    for i, flip in enumerate(rest):
        start = pl.multiple_of((group ^ flip) * block, LANES)
        kept[:, i * block : (i + 1) * block] = toks[:, pl.ds(start, block)]


def start_hidden(pieces, weights, flips, width):
    rows = pieces[0].shape[0]
    total = rows * len(pieces)
    block, cols = weights[0].shape
    left = width - block * len(flips)
    return pl.pallas_call(
        functools.partial(start_kernel, len(pieces), flips),
        out_shape=[pltpu.VMEM((total, cols), F32), pltpu.VMEM((total, left), BF16)],
        grid=(1,),
        in_specs=[pl.BlockSpec((rows, width), lambda i: (0, 0))] * len(pieces)
        + [pl.BlockSpec((block, cols), lambda i: (0, 0))] * len(weights),
        out_specs=[
            pl.BlockSpec((total, cols), lambda i: (0, 0)),
            pl.BlockSpec((total, left), lambda i: (0, 0)),
        ],
        scratch_shapes=[pltpu.VMEM((total, width), BF16)],
        compiler_params=pltpu.CompilerParams(vmem_limit_bytes=VMEM_BYTES),
        name="start_hidden",
    )(*[in_vmem(x) for x in [*pieces, *weights]])


def hidden_kernel(partial, rows, *refs):
    *weights, hidden = refs
    pre = partial[...]
    for i, ref in enumerate(weights):
        block = ref.shape[0]
        part = rows[:, i * block : (i + 1) * block]
        pre = pre + jnp.dot(part, ref[...], preferred_element_type=F32)
    gate, up, shared = (pre[:, i * LANES : (i + 1) * LANES] for i in range(3))
    hidden[:LANES, :] = (silu(gate) * up).T.astype(BF16)
    halves = (silu(shared) * swap_halves(shared)).T.astype(BF16)
    for parity in range(2):

        @pl.when(lax.rem(lax.axis_index("dp"), 2) == parity)
        def _():
            hidden[LANES:, :] = halves[parity * HALF : (parity + 1) * HALF]


def end_hidden(partial, rows, weights):
    args = [partial, rows, *weights]
    return pl.pallas_call(
        hidden_kernel,
        out_shape=pltpu.VMEM((partial.shape[1] // 2, rows.shape[0]), BF16),
        in_specs=[whole()] * len(args),
        compiler_params=pltpu.CompilerParams(vmem_limit_bytes=VMEM_BYTES),
        name="end_hidden",
    )(*[in_vmem(x) for x in args])


def scaled_kernel(start, *refs):
    *pieces, out = refs
    rows, block = pieces[0].shape[0], out.shape[1]
    blocks = []
    for piece in pieces:
        gates = piece[:, start + block :].astype(F32)
        lane = lax.broadcasted_iota(jnp.int32, gates.shape, 1)
        here = lane == lax.axis_index("expert")
        gate = jnp.sum(jnp.where(here, gates, 0.0), axis=1, keepdims=True)
        cot = piece[:, start : start + block].astype(F32)
        blocks.append((gate * cot).astype(BF16))
    out[...] = jnp.concatenate(blocks, axis=0)


def scaled_rows(pieces, width, block):
    total = pieces[0].shape[0] * len(pieces)
    return pl.pallas_call(
        functools.partial(scaled_kernel, width),
        out_shape=pltpu.VMEM((total, block), BF16),
        in_specs=[whole()] * len(pieces),
        compiler_params=pltpu.CompilerParams(vmem_limit_bytes=VMEM_BYTES),
        name="scaled_rows",
    )(*[in_vmem(x) for x in pieces])


def flip_kernel(*refs):
    half = len(refs) // 2
    for x, out in zip(refs[:half], refs[half:], strict=True):
        out[...] = x[...].T


def transposed(*arrays):
    return pl.pallas_call(
        flip_kernel,
        out_shape=[pltpu.VMEM(x.shape[::-1], x.dtype) for x in arrays],
        in_specs=[whole()] * len(arrays),
        compiler_params=pltpu.CompilerParams(vmem_limit_bytes=VMEM_BYTES),
        name="transposed",
    )(*arrays)


def update_kernel(flips, *refs):
    groups = lax.axis_size("dp")
    count = len(flips)
    hid_refs, (scaled, down, first, second), refs = refs[:count], refs[count : count + 4], refs[count + 4 :]
    outs, hidden = refs[:-1], refs[-1]
    cols = down.shape[0] // groups
    for i, ref in enumerate(hid_refs):
        hidden[i * cols : (i + 1) * cols, :] = ref[...]
    for chip_flip, out in enumerate(outs):
        tile = (lax.axis_index("expert") // CORES) ^ chip_flip
        lanes = pl.ds(pl.multiple_of(tile * LANES, LANES), LANES)
        grad = jnp.dot(hidden[...], scaled[:, lanes], preferred_element_type=F32)
        for i, flip in enumerate(flips):
            at = pl.multiple_of((lax.axis_index("dp") ^ flip) * cols, 16)
            here = pl.ds(at, cols), lanes
            part = grad[i * cols : (i + 1) * cols]
            out[i] = adam(down[here], first[here], second[here], part)


def update_tiles(hidden, flips, scaled, state, chips):
    cols, total = hidden[0].shape
    count = len(flips)
    return pl.pallas_call(
        functools.partial(update_kernel, flips),
        out_shape=[pltpu.VMEM((count, cols, scaled.shape[1] // chips), BF16)] * chips,
        in_specs=[whole()] * (count + 4),
        scratch_shapes=[pltpu.VMEM((count * cols, total), BF16)],
        compiler_params=pltpu.CompilerParams(vmem_limit_bytes=VMEM_BYTES),
        name="update_tiles",
    )(*[in_vmem(x) for x in [*hidden, scaled, *state]])


def regroup_kernel(*refs):
    chips = lax.axis_size("expert") // CORES
    tiles, outs = refs[:chips], refs[chips:]
    own = lax.axis_index("expert") // CORES
    for flip, tile in enumerate(tiles):
        for other, out in enumerate(outs):
            out[pl.ds(own ^ flip, 1)] = tile[other][None]


def regroup(tiles):
    groups, *tile = tiles[0].shape
    return pl.pallas_call(
        regroup_kernel,
        out_shape=[pltpu.VMEM((len(tiles), *tile), BF16)] * groups,
        in_specs=[whole()] * len(tiles),
        name="regroup",
    )(*[in_vmem(x) for x in tiles])


def pick_kernel(sets, order, *refs):
    count = sum(map(len, sets))
    kept, swapped, outs = refs[:count], refs[count : 2 * count], refs[2 * count :]
    chips = len(outs) // len(sets)
    spot = lax.axis_index("expert")
    core = lax.rem(spot, CORES)
    for flip in range(chips):
        source = order[spot ^ (flip * CORES)]
        chip, here = source // CORES, lax.rem(source, CORES) == core
        for blocks, chosen in ((kept, here), (swapped, jnp.logical_not(here))):

            @pl.when(chosen)
            def _():
                for n, flips in enumerate(sets):
                    for i, k in enumerate(flips):
                        outs[n * chips + flip][i] = blocks[k][chip]


def pick(order, kept, swapped, sets):
    chips, *tile = kept[0].shape
    return pl.pallas_call(
        functools.partial(pick_kernel, sets),
        out_shape=[pltpu.VMEM((len(flips), *tile), BF16) for flips in sets for _ in range(chips)],
        in_specs=[smem()] + [whole()] * (2 * len(kept)),
        compiler_params=pltpu.CompilerParams(vmem_limit_bytes=VMEM_BYTES),
        name="pick",
    )(order, *[in_vmem(x) for x in [*kept, *swapped]])


def unpack_kernel(flips, *refs):
    chips = lax.axis_size("expert") // CORES
    pieces, (out, sems) = refs[:chips], refs[-2:]
    block = out.shape[2] // lax.axis_size("dp")
    copies = []
    for i, piece in enumerate(pieces):
        tile = (lax.axis_index("expert") // CORES) ^ i
        for j, flip in enumerate(flips):
            left = (lax.axis_index("dp") ^ flip) * block + tile * LANES
            lanes = pl.ds(pl.multiple_of(left, LANES), LANES)
            copies.append(
                pltpu.make_async_copy(piece.at[j], out.at[0, :, lanes], sems.at[len(copies)])
            )
    for copy in copies:
        copy.start()
    for copy in copies:
        copy.wait()


def unpack(pieces, flips, width, cols, out):
    given = [] if out is None else [out]
    anywhere = pl.BlockSpec(memory_space=pl.ANY)
    return pl.pallas_call(
        functools.partial(unpack_kernel, flips),
        out_shape=jax.ShapeDtypeStruct((1, cols, width), BF16),
        in_specs=[whole()] * len(pieces) + [anywhere] * len(given),
        out_specs=anywhere,
        scratch_shapes=[pltpu.SemaphoreType.DMA((len(pieces) * len(flips),))],
        input_output_aliases={len(pieces): 0} if given else {},
        name="unpack",
    )(*[in_vmem(x) for x in pieces], *given)


def dense(tokens, cotangent, route_ids, route_gates, gate_up, down, moment1, moment2, placement):
    experts = lax.axis_size("expert")
    groups = lax.axis_size("dp")
    width = tokens.shape[1]
    units = down.shape[2]
    block = width // groups

    own, near, far, farthest = pack_weights(gate_up[0], groups)
    sent = pack_rows(tokens, cotangent, route_ids, route_gates, groups)
    blocks = [sent[0]] + [partner(sent[k], "dp", k) for k in range(1, groups)]
    state = transposed(down[0], moment1[0], moment2[0])
    plane = order_groups([after(blocks[0], state[0]), *blocks[1:]])
    chips = [plane] + [partner(plane, "expert", k) for k in range(2, experts, 2)]
    pieces = chips + [partner(x, "expert", 1) for x in chips]
    far = partner(after(far, blocks[1]), "dp", 2)
    near = partner(after(near, chips[1]), "dp", 1)
    farthest = partner(after(farthest, far), "dp", 3)

    cols = units // groups
    partial, rows = start_hidden(pieces, [own, far, near], (0, 2, 1), width)
    part = end_hidden(partial, rows, [farthest])
    scaled = scaled_rows(pieces, width, block)
    across = partner(part, "dp", 2)
    hidden = [part, partner(part, "dp", 1), across, partner(across, "dp", 1)]
    planes = experts // CORES
    kept = {}
    for flips in ((0, 3), (1, 2)):
        tiles = update_tiles([hidden[k] for k in flips], flips, scaled, state, planes)
        tiles = [tiles[0]] + [
            partner(tiles[k], "expert", k * CORES) for k in range(1, planes)
        ]
        for k, x in zip(flips, regroup(tiles), strict=True):
            kept[k] = partner(x, "dp", k) if k else x
    swapped = {k: partner(x, "expert", 1) for k, x in kept.items()}
    sets = ((1, 0), (3, 2))
    every = range(groups)
    chosen = pick(placement, [kept[k] for k in every], [swapped[k] for k in every], sets)
    out = None
    for n, flips in enumerate(sets):
        picked = chosen[n * planes : (n + 1) * planes]
        landed = [picked[0]] + [
            partner(picked[k], "expert", k * CORES) for k in range(1, planes)
        ]
        out = unpack(landed, flips, width, cols, out)
    return out.transpose(0, 2, 1)


def shards(tokens, cotangent, route_ids, *rest):
    every = route_ids.shape[1] == lax.axis_size("expert")
    return (dense if every else routed)(tokens, cotangent, route_ids, *rest)


def solution(mesh):
    placed = (
        P(("expert", "dp"), None),
        P(("expert", "dp"), None),
        P(("expert", "dp"), None),
        P(("expert", "dp"), None),
        P("expert", "dp", None),
        P("expert", "dp", None),
        P("expert", "dp", None),
        P("expert", "dp", None),
        P(),
    )
    return jax.shard_map(
        shards, mesh=mesh, in_specs=placed, out_specs=P("expert", None, "dp"), check_vma=False
    )
```
